1024 devices in a mesh: shard: 32 (over z), replica: 32 (over x, y, core).
Axes of the slice: x: 4, y: 4, z: 32, core: 2. Of those that a mesh axis runs over, the one named last changes fastest.
Arguments:
- ids: int32 [262144, 4], P(('shard', 'replica')), may hold values from 0 to 32767, as said below
- pooled: bfloat16 [262144, 256], P(('shard', 'replica')), may hold values from -6 to 6
- pre_act: bfloat16 [262144, 512], P(('shard', 'replica')), may hold values from -6 to 6
- grad_out: bfloat16 [262144, 512], P(('shard', 'replica')), may hold values from -6 to 6
- w_top: bfloat16 [256, 512], replicated, may hold values from -0.375 to 0.375
- table: float32 [32768, 256], P('shard'), may hold values from -6 to 6
- accum: float32 [32768], P('shard'), may hold values from 0.1 to 10
Outputs:
- new_table: float32 [32768, 256], P('shard')
- new_accum: float32 [32768], P('shard')
- grad_top: float32 [256, 512], replicated
The draws below stay inside these ranges and needn't reach their ends.
Inputs may be any that keep to these rules, and one draw needn't show every extreme that they name: `ids`: row i is owned by shard index i // 1024. Among the 1024 lookups of one device (its aligned block of 256 samples), at most 64 name rows of one owner, and in every such block some owner is named exactly 64 times.
All inputs are finite; a program needn't handle non-finite values.
Results may differ from the reference program's by a relative error of at most 0.0031.
Values may be sent and summed in bfloat16 or wider, within the bound.
No kernel may reach another device: no remote copies, remote signals or barrier semaphores. Data moves between devices by JAX's collectives and lax.ppermute only.
A program may use at most 32 MiB of HBM per device.

```python
import math
import jax
import jax.numpy as jnp
from jax import lax

E = 256
H = 512
ROWS_DEV = 1024
B_DEV = 256
LOOKUPS = 4
CAP = 64
ROWS = 32768
SAMPLES = 262144
N_SHARD = 32
N_REPLICA = 32


def draw_ids(key, part):
    key = jax.random.fold_in(key, 11)
    block_total = N_SHARD * N_REPLICA
    lookup_count = B_DEV * LOOKUPS
    slot_total = N_SHARD * CAP
    random_keys = jax.random.split(key, 6)
    extra_credit = jax.random.randint(random_keys[0], (block_total, N_SHARD), 0, 4000)
    hottest = jax.random.randint(random_keys[1], (block_total,), 0, N_SHARD)
    slot_holder = jnp.arange(slot_total, dtype=jnp.int32) // CAP
    random_jitter = jax.random.randint(random_keys[2], (block_total, slot_total), 0, 4000)
    rank_score = random_jitter + jnp.take_along_axis(extra_credit, jnp.broadcast_to(slot_holder[None, :], (block_total, slot_total)), axis=1)
    rank_score = rank_score + jnp.where(slot_holder[None, :] == hottest[:, None], 100000, 0)
    distinct = rank_score * slot_total + jnp.arange(slot_total, dtype=jnp.int32)[None, :]
    chosen_vals, chosen = jax.lax.top_k(distinct, lookup_count)
    owner_of = chosen // CAP
    order_keys = jax.random.randint(random_keys[3], (block_total, lookup_count), 0, 65536)
    order_keys = order_keys * lookup_count + jnp.arange(lookup_count, dtype=jnp.int32)[None, :]
    shuffle = jnp.argsort(order_keys, axis=1)
    owner_of = jnp.take_along_axis(owner_of, shuffle, axis=1)
    first_draw = jax.random.randint(random_keys[4], (block_total, lookup_count), 0, ROWS_DEV)
    second_draw = jax.random.randint(random_keys[5], (block_total, lookup_count), 0, ROWS_DEV)
    row_local = first_draw * second_draw // ROWS_DEV
    row_ids = owner_of * ROWS_DEV + row_local
    return row_ids.reshape(SAMPLES, LOOKUPS).astype(jnp.int32)


def levels(key, dims, pieces, least, high):
    def one(position, parts):
        heights = jax.random.uniform(jax.random.fold_in(jax.random.fold_in(key, 6), position), (parts,), jnp.float32, least / len(pieces), high / len(pieces))
        return jnp.repeat(jnp.exp(heights), dims[position] // parts).reshape((-1,) + (1,) * (len(dims) - position - 1))

    gain = one(*pieces[0])
    for cut in pieces[1:]:
        gain = gain * one(*cut)
    return gain


def noise(rng, shape, spread, bound, shards=(), kind=jnp.bfloat16):
    drawn = jax.random.normal(rng, shape, jnp.float32) * spread
    if len(shards) > 0:
        drawn = levels(rng, shape, shards, -0.22, 0.18) * drawn
    return jnp.clip(drawn, min=-bound, max=bound).astype(kind)


def setup_inputs(seed: int = 0) -> dict:
    splits = jax.random.split(jax.random.key(seed), 8)
    return {
        "ids": draw_ids(jax.random.fold_in(splits[7], 71), 0),
        "pooled": noise(splits[1], (SAMPLES, E), 1.0, 6.0, ((0, 1024),)),
        "pre_act": noise(splits[2], (SAMPLES, H), 1.5, 6.0, ((0, 1024),)),
        "grad_out": noise(splits[3], (SAMPLES, H), 1.0, 6.0, ((0, 1024),)),
        "w_top": noise(splits[4], (E, H), E ** -0.5, 0.375),
        "table": noise(splits[5], (ROWS, E), 1.0, 6.0, ((0, 32),), jnp.float32),
        "accum": jnp.clip(jnp.exp(math.log(10.0) - 4.6051702 * jax.random.uniform(splits[6], (ROWS,), jnp.float32) ** levels(splits[6], (ROWS,), ((0, 32),), -0.2, 0.2)), 0.1, 10.0),
    }


LEARN_RATE = 0.5
ADA_EPS = 1e-08

def reference(ids, pooled, pre_act, grad_out, w_top, table, accum):
    tanh_pre = jnp.tanh(pre_act.astype(jnp.float32))
    derivative = (grad_out.astype(jnp.float32) * (1.0 - tanh_pre * tanh_pre)).astype(jnp.bfloat16)
    grad_pooled = jnp.dot(derivative, w_top.T, preferred_element_type=jnp.float32).astype(jnp.bfloat16)
    grad_top = jnp.dot(pooled.T, derivative, preferred_element_type=jnp.float32)
    pooled_grad32 = grad_pooled.astype(jnp.float32)
    row_grad = jnp.zeros((ROWS, E), jnp.float32)
    for column in range(LOOKUPS):
        row_grad = row_grad + jax.ops.segment_sum(pooled_grad32, ids[:, column], num_segments=ROWS)
    new_accum = accum + lax.optimization_barrier(jnp.mean(row_grad * row_grad, axis=1))
    new_table = table - LEARN_RATE * row_grad / (jnp.sqrt(new_accum)[:, None] + ADA_EPS)
    return (new_table, new_accum, grad_top)
```

```python
import jax
import jax.numpy as jnp
from jax import lax
from jax.experimental import pallas as pl
from jax.experimental.pallas import tpu as pltpu
from jax.sharding import PartitionSpec as P

LEARN_RATE = 0.5
ADA_EPS = 1e-08

BF16 = jnp.bfloat16
F32 = jnp.float32

PLANE = 32
COLS = 8
NEAR = 4
FAR = 8
LOW = 256
HIGH = 128
VMEM_BYTES = 40 * 1024 * 1024


def call(body, out_shape, args, scratch=()):
    return pl.pallas_call(
        body,
        out_shape=out_shape,
        in_specs=[pl.BlockSpec(memory_space=pltpu.VMEM)] * len(args),
        out_specs=jax.tree.map(lambda _: pl.BlockSpec(memory_space=pltpu.VMEM), out_shape),
        scratch_shapes=list(scratch),
        compiler_params=pltpu.CompilerParams(vmem_limit_bytes=VMEM_BYTES),
    )(*args)


def local_grads(ids_ref, pooled_ref, pre_ref, grad_ref, w_ref, out_ref):
    tanh_pre = jnp.tanh(pre_ref[...].astype(F32))
    derivative = (grad_ref[...].astype(F32) * (1.0 - tanh_pre * tanh_pre)).astype(BF16)
    pooled_t = lax.dot_general(
        w_ref[...], derivative, (((1,), (1,)), ((), ())), preferred_element_type=F32
    )
    dense = lax.dot_general(
        pooled_ref[...], derivative, (((0,), (0,)), ((), ())), preferred_element_type=F32
    )
    samples = pooled_t.shape[1]
    ids = ids_ref[...]
    digits = jnp.concatenate([ids // LOW, ids % LOW], axis=0).astype(F32)
    shape = (PLANE, COLS, samples)
    left = dense[:, :samples].reshape(shape)
    right = dense[:, samples:].reshape(shape)
    out_ref[:, 0:16, :] = jnp.concatenate([pooled_t.reshape(shape), left], axis=1).astype(BF16)
    out_ref[:, 16:32, :] = jnp.concatenate(
        [right, jnp.broadcast_to(digits[None], shape)], axis=1
    ).astype(BF16)


def merge_rows(got_ref, out_ref, high_ref, low_ref, total_ref):
    samples = got_ref.shape[2]
    lookups = 4
    total_ref[...] = jnp.zeros_like(total_ref)
    second = (lax.broadcasted_iota(jnp.int32, (16, samples), 0) >= 8).astype(F32)
    low_iota = lax.broadcasted_iota(jnp.int32, (LOW, samples), 0).astype(F32).astype(BF16)

    def step(source, dense):
        block = got_ref[source].astype(F32)
        grad = block[0:8]
        grad = jnp.concatenate([grad, grad], axis=0).astype(BF16)
        for j in range(lookups):
            lanes = slice(j * samples, (j + 1) * samples)
            high = (jnp.broadcast_to(block[24 + j : 25 + j], (16, samples)) - second).astype(BF16)
            low = jnp.broadcast_to(block[28 + j : 29 + j], (LOW, samples)).astype(BF16)
            for k in range(HIGH // 2):
                high_ref[16 * k : 16 * k + 16, lanes] = jnp.where(
                    high == jnp.asarray(2 * k, BF16), grad, jnp.zeros_like(grad)
                )
            low_ref[:, lanes] = jnp.where(
                low == low_iota, jnp.ones_like(low), jnp.zeros_like(low)
            )
        total_ref[...] += lax.dot_general(
            high_ref[...], low_ref[...], (((1,), (1,)), ((), ())), preferred_element_type=F32
        )
        return dense + block[8:24]

    dense = lax.fori_loop(0, PLANE, step, jnp.zeros((16, samples), F32))
    big = dense.astype(BF16)
    small = (dense - big.astype(F32)).astype(BF16)
    rows = total_ref[...].astype(BF16).reshape(FAR, NEAR, 32, LOW)
    for near in range(NEAR):
        out_ref[near, 0 : FAR * 32, :] = rows[:, near].reshape(FAR * 32, LOW)
        out_ref[near, FAR * 32 : FAR * 32 + 16, :] = big
        out_ref[near, FAR * 32 + 16 : FAR * 32 + 32, :] = small


def merge_near(got_ref, out_ref):
    total = jnp.sum(got_ref[...].astype(F32), axis=0)
    rows = total[: FAR * 32].reshape(FAR, 32, LOW)
    dense = total[FAR * 32 : FAR * 32 + 16] + total[FAR * 32 + 16 :]
    out_ref[:, 0:32, :] = rows.astype(BF16)
    out_ref[:, 32:48, :] = jnp.broadcast_to(dense.astype(BF16)[None], (FAR, 16, LOW))


def merge_far(got_ref, out_ref):
    total = jnp.sum(got_ref[...].astype(F32), axis=0).astype(BF16)
    out_ref[...] = jnp.broadcast_to(total[None], out_ref.shape)


def update_rows(got_ref, table_ref, accum_ref, table_out, accum_out, top_out):
    width = table_ref.shape[1]
    for h in range(4):
        rows = got_ref[:, 8 * h : 8 * h + 8, :].astype(F32).reshape(width, LOW)
        squares = jnp.sum(rows * rows, axis=0, keepdims=True) * (1.0 / width)
        scaled = []
        for half in range(2):
            lanes = slice(128 * half, 128 * half + 128)
            at = slice(2 * h + half, 2 * h + half + 1)
            new_accum = accum_ref[at, :] + squares[:, lanes]
            accum_out[at, :] = new_accum
            scaled.append(rows[:, lanes] * (LEARN_RATE / (jnp.sqrt(new_accum) + ADA_EPS)))
        change = jnp.concatenate(scaled, axis=1).T
        at = slice(h * LOW, (h + 1) * LOW)
        table_out[at, :] = table_ref[at, :] - change
    top_out[:, :LOW] = got_ref[:, 32:40, :].astype(F32).reshape(width, LOW)
    top_out[:, LOW:] = got_ref[:, 40:48, :].astype(F32).reshape(width, LOW)


def exchange(parts, axis, groups=None):
    return lax.all_to_all(
        parts, axis, split_axis=0, concat_axis=0, tiled=True, axis_index_groups=groups
    )


def local(ids, pooled, pre_act, grad_out, w_top, table, accum):
    samples = pooled.shape[0]
    near_groups = [[f * NEAR + n for n in range(NEAR)] for f in range(FAR)]
    far_groups = [[f * NEAR + n for f in range(FAR)] for n in range(NEAR)]
    sent = call(
        local_grads,
        jax.ShapeDtypeStruct((PLANE, 32, samples), BF16),
        (ids.T, pooled, pre_act, grad_out, w_top),
    )
    got = exchange(sent, "replica")
    merged = call(
        merge_rows,
        jax.ShapeDtypeStruct((NEAR, FAR * 32 + 32, LOW), BF16),
        (got,),
        scratch=(
            pltpu.VMEM((HIGH * COLS, 4 * samples), BF16),
            pltpu.VMEM((LOW, 4 * samples), BF16),
            pltpu.VMEM((HIGH * COLS, LOW), F32),
        ),
    )
    got = exchange(merged, "shard", near_groups)
    merged = call(merge_near, jax.ShapeDtypeStruct((FAR, 48, LOW), BF16), (got,))
    got = exchange(merged, "shard", far_groups)
    merged = call(merge_far, jax.ShapeDtypeStruct((PLANE, 48, LOW), BF16), (got,))
    got = exchange(merged, "replica")
    rows = table.shape[0]
    new_table, new_accum, grad_top = call(
        update_rows,
        (
            jax.ShapeDtypeStruct(table.shape, F32),
            jax.ShapeDtypeStruct((rows // 128, 128), F32),
            jax.ShapeDtypeStruct(w_top.shape, F32),
        ),
        (got, table, accum.reshape(rows // 128, 128)),
    )
    return (new_table, new_accum.reshape(rows), grad_top)


def solution(mesh):
    return jax.shard_map(
        local,
        mesh=mesh,
        in_specs=(
            P(("shard", "replica"), None),
            P(("shard", "replica"), None),
            P(("shard", "replica"), None),
            P(("shard", "replica"), None),
            P(),
            P("shard", None),
            P("shard"),
        ),
        out_specs=(P("shard", None), P("shard"), P()),
        check_vma=False,
    )
```

```python
import jax
import jax.numpy as jnp
from jax import lax
from jax.experimental import pallas as pl
from jax.experimental.pallas import tpu as pltpu
from jax.sharding import PartitionSpec as P

LEARN_RATE = 0.5
ADA_EPS = 1e-08

BF16 = jnp.bfloat16
F32 = jnp.float32

PLANE = 32
COLS = 8
NEAR = 4
FAR = 8
LOW = 256
HIGH = 128
VMEM_BYTES = 40 * 1024 * 1024


def call(body, out_shape, args, scratch=(), memory=pltpu.VMEM, cost=None, vmem=VMEM_BYTES):
    return pl.pallas_call(
        body,
        out_shape=out_shape,
        in_specs=[pl.BlockSpec(memory_space=memory)] * len(args),
        out_specs=jax.tree.map(lambda _: pl.BlockSpec(memory_space=pltpu.VMEM), out_shape),
        scratch_shapes=list(scratch),
        cost_estimate=cost,
        compiler_params=pltpu.CompilerParams(vmem_limit_bytes=vmem),
    )(*args)


def local_grads(
    ids_hbm, pooled_hbm, pre_hbm, grad_hbm, w_hbm, out_ref, ids_ref, pooled_ref, pre_ref, grad_ref, w_ref, sems
):
    pairs = (
        (pre_hbm, pre_ref),
        (grad_hbm, grad_ref),
        (w_hbm, w_ref),
        (pooled_hbm, pooled_ref),
        (ids_hbm, ids_ref),
    )
    copies = [
        pltpu.make_async_copy(source, target, sems.at[i])
        for i, (source, target) in enumerate(pairs)
    ]
    for copy in copies:
        copy.start()
    copies[0].wait()
    tanh_pre = jnp.tanh(pre_ref[...].astype(F32))
    copies[1].wait()
    derivative = (grad_ref[...].astype(F32) * (1.0 - tanh_pre * tanh_pre)).astype(BF16)
    copies[2].wait()
    pooled_t = lax.dot_general(
        w_ref[...], derivative, (((1,), (1,)), ((), ())), preferred_element_type=F32
    )
    copies[3].wait()
    dense = lax.dot_general(
        pooled_ref[...], derivative, (((0,), (0,)), ((), ())), preferred_element_type=F32
    )
    copies[4].wait()
    samples = pooled_t.shape[1]
    ids = ids_ref[...]
    digits = jnp.concatenate([ids // LOW, ids % LOW], axis=0).astype(F32)
    shape = (PLANE, COLS, samples)
    left = dense[:, :samples].reshape(shape)
    right = dense[:, samples:].reshape(shape)
    out_ref[:, 0:16, :] = jnp.concatenate([pooled_t.reshape(shape), left], axis=1).astype(BF16)
    out_ref[:, 16:32, :] = jnp.concatenate(
        [right, jnp.broadcast_to(digits[None], shape)], axis=1
    ).astype(BF16)


def merge_dense(got_ref, out_ref):
    total = jnp.zeros((32, got_ref.shape[2]), F32)
    for source in range(PLANE):
        total += got_ref[source].astype(F32)
    out_ref[...] = jnp.broadcast_to(total[8:24].astype(BF16)[None], out_ref.shape)


def merge_rows(got_ref, out_ref, high_ref, low_ref, total_ref):
    samples = got_ref.shape[2]
    lookups = 4
    total_ref[...] = jnp.zeros_like(total_ref)
    second = (lax.broadcasted_iota(jnp.int32, (16, samples), 0) >= 8).astype(F32)
    low_iota = lax.broadcasted_iota(jnp.int32, (LOW, samples), 0).astype(F32).astype(BF16)

    def step(pair, carry):
        for half in range(2):
            block = got_ref[2 * pair + half].astype(F32)
            grad = block[0:8]
            grad = jnp.concatenate([grad, grad], axis=0).astype(BF16)
            for j in range(lookups):
                first = (half * lookups + j) * samples
                lanes = slice(first, first + samples)
                high = (jnp.broadcast_to(block[24 + j : 25 + j], (16, samples)) - second).astype(
                    BF16
                )
                low = jnp.broadcast_to(block[28 + j : 29 + j], (LOW, samples)).astype(BF16)
                for k in range(HIGH // 2):
                    high_ref[16 * k : 16 * k + 16, lanes] = jnp.where(
                        high == jnp.asarray(2 * k, BF16), grad, jnp.zeros_like(grad)
                    )
                low_ref[:, lanes] = jnp.where(
                    low == low_iota, jnp.ones_like(low), jnp.zeros_like(low)
                )
        total_ref[...] += lax.dot_general(
            high_ref[...], low_ref[...], (((1,), (1,)), ((), ())), preferred_element_type=F32
        )
        return carry

    lax.fori_loop(0, PLANE // 2, step, 0)
    rows = total_ref[...].astype(BF16).reshape(FAR, NEAR, 32, LOW)
    for near in range(NEAR):
        out_ref[near] = rows[:, near].reshape(FAR * 32, LOW)


def join_dense(rows_ref, dense_ref, out_ref):
    dense = jnp.sum(dense_ref[...].astype(F32), axis=0)
    big = dense.astype(BF16)
    small = (dense - big.astype(F32)).astype(BF16)
    count = FAR * 32
    out_ref[:, :count, :] = rows_ref[...]
    for near in range(NEAR):
        out_ref[near, count : count + 16, :] = big
        out_ref[near, count + 16 : count + 32, :] = small


def merge_near(got_ref, rows_ref, dense_ref):
    total = jnp.sum(got_ref[...].astype(F32), axis=0)
    count = FAR * 32
    rows_ref[...] = total[:count].reshape(FAR, 32, LOW).astype(BF16)
    dense_ref[...] = (total[count : count + 16] + total[count + 16 :]).astype(BF16)


def merge_far(got_ref, dense_ref, out_ref):
    total = jnp.sum(got_ref[...].astype(F32), axis=0).astype(BF16)
    out_ref[:, 0:32, :] = jnp.broadcast_to(total[None], (PLANE, 32, LOW))
    out_ref[:, 32:48, :] = jnp.broadcast_to(dense_ref[...][None], (PLANE, 16, LOW))


def update_rows(got_ref, table_ref, accum_ref, table_out, accum_out, top_out):
    width = table_ref.shape[1]
    for h in range(4):
        rows = got_ref[:, 8 * h : 8 * h + 8, :].astype(F32).reshape(width, LOW)
        squares = jnp.sum(rows * rows, axis=0, keepdims=True) * (1.0 / width)
        scaled = []
        for half in range(2):
            lanes = slice(128 * half, 128 * half + 128)
            at = slice(2 * h + half, 2 * h + half + 1)
            new_accum = accum_ref[at, :] + squares[:, lanes]
            accum_out[at, :] = new_accum
            scaled.append(rows[:, lanes] * (LEARN_RATE / (jnp.sqrt(new_accum) + ADA_EPS)))
        change = jnp.concatenate(scaled, axis=1).T
        at = slice(h * LOW, (h + 1) * LOW)
        table_out[at, :] = table_ref[at, :] - change
    top_out[:, :LOW] = got_ref[:, 32:40, :].astype(F32).reshape(width, LOW)
    top_out[:, LOW:] = got_ref[:, 40:48, :].astype(F32).reshape(width, LOW)


def exchange(parts, axis, groups=None):
    return lax.all_to_all(
        parts, axis, split_axis=0, concat_axis=0, tiled=True, axis_index_groups=groups
    )


def local(ids, pooled, pre_act, grad_out, w_top, table, accum):
    samples = pooled.shape[0]
    near_groups = [[f * NEAR + n for n in range(NEAR)] for f in range(FAR)]
    far_groups = [[f * NEAR + n for f in range(FAR)] for n in range(NEAR)]
    sent = call(
        local_grads,
        jax.ShapeDtypeStruct((PLANE, 32, samples), BF16),
        (ids.T, pooled, pre_act, grad_out, w_top),
        scratch=[pltpu.VMEM(a.shape, a.dtype) for a in (ids.T, pooled, pre_act, grad_out, w_top)]
        + [pltpu.SemaphoreType.DMA((5,))],
        memory=pl.ANY,
        vmem=64 * 1024 * 1024 - 256 * 1024,
    )
    got = exchange(sent, "replica")
    dense = call(merge_dense, jax.ShapeDtypeStruct((FAR, 16, LOW), BF16), (got,))
    dense = exchange(dense, "shard", far_groups)
    merged = call(
        merge_rows,
        jax.ShapeDtypeStruct((NEAR, FAR * 32, LOW), BF16),
        (got,),
        scratch=(
            pltpu.VMEM((HIGH * COLS, 8 * samples), BF16),
            pltpu.VMEM((LOW, 8 * samples), BF16),
            pltpu.VMEM((HIGH * COLS, LOW), F32),
        ),
        cost=pl.CostEstimate(flops=17_200_000_000, bytes_accessed=1_000_000, transcendentals=0),
    )
    merged = call(
        join_dense, jax.ShapeDtypeStruct((NEAR, FAR * 32 + 32, LOW), BF16), (merged, dense)
    )
    got = exchange(merged, "shard", near_groups)
    merged, dense = call(
        merge_near,
        (
            jax.ShapeDtypeStruct((FAR, 32, LOW), BF16),
            jax.ShapeDtypeStruct((16, LOW), BF16),
        ),
        (got,),
    )
    got = exchange(merged, "shard", far_groups)
    merged = call(merge_far, jax.ShapeDtypeStruct((PLANE, 48, LOW), BF16), (got, dense))
    got = exchange(merged, "replica")
    rows = table.shape[0]
    new_table, new_accum, grad_top = call(
        update_rows,
        (
            jax.ShapeDtypeStruct(table.shape, F32),
            jax.ShapeDtypeStruct((rows // 128, 128), F32),
            jax.ShapeDtypeStruct(w_top.shape, F32),
        ),
        (got, table, accum.reshape(rows // 128, 128)),
    )
    return (new_table, new_accum.reshape(rows), grad_top)


def solution(mesh):
    return jax.shard_map(
        local,
        mesh=mesh,
        in_specs=(
            P(("shard", "replica"), None),
            P(("shard", "replica"), None),
            P(("shard", "replica"), None),
            P(("shard", "replica"), None),
            P(),
            P("shard", None),
            P("shard"),
        ),
        out_specs=(P("shard", None), P("shard"), P()),
        check_vma=False,
    )
```

```python
import jax
import jax.numpy as jnp
from jax import lax
from jax.experimental import pallas as pl
from jax.experimental.pallas import tpu as pltpu
from jax.sharding import PartitionSpec as P

LEARN_RATE = 0.5
ADA_EPS = 1e-08

BF16 = jnp.bfloat16
F32 = jnp.float32

PLANE = 32
COLS = 8
NEAR = 4
FAR = 8
LOW = 256
TILES = 8
OWNERS = 4
CAP = 64
HIGH = 16
VMEM_BYTES = 40 * 1024 * 1024


def call(body, out_shape, args, scratch=(), memory=pltpu.VMEM, cost=None, vmem=VMEM_BYTES):
    return pl.pallas_call(
        body,
        out_shape=out_shape,
        in_specs=[pl.BlockSpec(memory_space=memory)] * len(args),
        out_specs=jax.tree.map(lambda _: pl.BlockSpec(memory_space=pltpu.VMEM), out_shape),
        scratch_shapes=list(scratch),
        cost_estimate=cost,
        compiler_params=pltpu.CompilerParams(vmem_limit_bytes=vmem),
    )(*args)


def code(number):
    size = (number & 127).astype(F32) * (1.0 / 128.0) + 1.0
    return jnp.where(number >= 128, -size, size)


def local_grads(
    ids_hbm, pooled_hbm, pre_hbm, grad_hbm, w_hbm, out_ref, ids_ref, pooled_ref, pre_ref, grad_ref, w_ref, sems
):
    pairs = (
        (pre_hbm, pre_ref),
        (grad_hbm, grad_ref),
        (w_hbm, w_ref),
        (pooled_hbm, pooled_ref),
        (ids_hbm, ids_ref),
    )
    copies = [
        pltpu.make_async_copy(source, target, sems.at[i])
        for i, (source, target) in enumerate(pairs)
    ]
    for copy in copies:
        copy.start()
    copies[0].wait()
    tanh_pre = jnp.tanh(pre_ref[...].astype(F32))
    copies[1].wait()
    derivative = (grad_ref[...].astype(F32) * (1.0 - tanh_pre * tanh_pre)).astype(BF16)
    copies[2].wait()
    pooled_t = lax.dot_general(
        w_ref[...], derivative, (((1,), (1,)), ((), ())), preferred_element_type=F32
    )
    copies[3].wait()
    dense = lax.dot_general(
        pooled_ref[...], derivative, (((0,), (0,)), ((), ())), preferred_element_type=F32
    )
    copies[4].wait()
    samples = pooled_t.shape[1]
    lookups = ids_ref.shape[0]
    ids = jnp.concatenate([ids_ref[j : j + 1, :] for j in range(lookups)], axis=1)
    owner = ids >> 10
    total = lookups * samples
    named = lax.broadcasted_iota(jnp.int32, (PLANE, total), 0) == owner
    before = (
        lax.broadcasted_iota(jnp.int32, (samples, samples), 0)
        < lax.broadcasted_iota(jnp.int32, (samples, samples), 1)
    ).astype(F32).astype(BF16)
    named = named.astype(F32)
    ranks = []
    carry = jnp.zeros((PLANE, 1), F32)
    for j in range(lookups):
        part = named[:, j * samples : (j + 1) * samples]
        earlier = carry + jnp.dot(part.astype(BF16), before, preferred_element_type=F32)
        ranks.append(jnp.sum(part * earlier, axis=0, keepdims=True))
        carry += jnp.sum(part, axis=1, keepdims=True)
    slot = ((owner & 3) * CAP).astype(F32) + jnp.concatenate(ranks, axis=1)
    place = code(ids & (LOW - 1)) * (1 << ((ids >> 8) & (HIGH - 1))).astype(F32)
    number = code(lax.broadcasted_iota(jnp.int32, (1, total), 1) & (samples - 1))
    tile = (lax.broadcasted_iota(jnp.int32, (TILES, total), 0) == (owner >> 2)).astype(F32)
    at_slot = (
        lax.broadcasted_iota(jnp.int32, (OWNERS * CAP, total), 0).astype(F32) == slot
    )
    tables = [
        lax.dot_general(
            tile.astype(BF16),
            jnp.where(at_slot, value, 0.0).astype(BF16),
            (((1,), (1,)), ((), ())),
            preferred_element_type=F32,
        )
        for value in (place, number)
    ]
    shape = (PLANE, COLS, samples)
    left = dense[:, :samples].reshape(shape)
    right = dense[:, samples:].reshape(shape)
    out_ref[:, 0:16, :] = jnp.concatenate([left, right], axis=1).astype(BF16)
    out_ref[:, 16:32, :] = jnp.broadcast_to(
        jnp.concatenate(tables, axis=0).astype(BF16)[None], (PLANE, 16, samples)
    )
    out_ref[:, 32:40, :] = pooled_t.reshape(shape).astype(BF16)


def merge_rows(got_ref, out_ref, high_ref, low_ref, total_ref):
    samples = got_ref.shape[2]
    batch = high_ref.shape[1] // samples
    slots = OWNERS * CAP
    total_ref[...] = jnp.zeros_like(total_ref)
    second = (lax.broadcasted_iota(jnp.int32, (16, slots), 0) >= 8).astype(F32)
    low_iota = lax.broadcasted_iota(jnp.int32, (LOW, slots), 0).astype(F32).astype(BF16)

    def step(group, dense):
        for member in range(batch):
            source = group * batch + member
            dense += got_ref[source, 0:16, :].astype(F32)
            table = got_ref[source, 16:32, :].astype(F32)
            grad = got_ref[source, 32:40, :].astype(F32)
            place = jnp.abs(table[:TILES])
            number = jnp.abs(table[TILES:])
            upper = table[TILES:] < 0.0
            lane = jnp.maximum((number - 1.0) * 128.0, 0.0).astype(jnp.int32)
            filled = number > 0.0
            high = jnp.zeros_like(place)
            scale = jnp.ones_like(place)
            for k in range(1, HIGH):
                above = place >= float(1 << k)
                high = jnp.where(above, float(k), high)
                scale = jnp.where(above, 1.0 / (1 << k), scale)
            low = (place * scale - 1.0) * 128.0 + jnp.where(table[:TILES] < 0.0, 128.0, 0.0)
            lanes = slice(member * slots, (member + 1) * slots)
            for t in range(TILES):
                halves = []
                for half in range(0, slots, 128):
                    at = jnp.broadcast_to(lane[t : t + 1, half : half + 128], (COLS, 128))
                    taken = [
                        jnp.take_along_axis(grad[:, first : first + 128], at, axis=1)
                        for first in range(0, samples, 128)
                    ]
                    value = jnp.where(upper[t : t + 1, half : half + 128], taken[1], taken[0])
                    halves.append(jnp.where(filled[t : t + 1, half : half + 128], value, 0.0))
                value = jnp.concatenate(halves, axis=1)
                value = jnp.concatenate([value, value], axis=0).astype(BF16)
                which = (jnp.broadcast_to(high[t : t + 1], (16, slots)) - second).astype(BF16)
                rows = HIGH * COLS * t
                for k in range(HIGH // 2):
                    high_ref[rows + 16 * k : rows + 16 * k + 16, lanes] = jnp.where(
                        which == jnp.asarray(2 * k, BF16), value, jnp.zeros_like(value)
                    )
                digit = jnp.broadcast_to(low[t : t + 1], (LOW, slots)).astype(BF16)
                low_ref[t * LOW : (t + 1) * LOW, lanes] = jnp.where(
                    digit == low_iota, jnp.ones_like(digit), jnp.zeros_like(digit)
                )
        for t in range(TILES):
            rows = slice(HIGH * COLS * t, HIGH * COLS * (t + 1))
            total_ref[rows, :] += lax.dot_general(
                high_ref[rows, :],
                low_ref[t * LOW : (t + 1) * LOW, :],
                (((1,), (1,)), ((), ())),
                preferred_element_type=F32,
            )
        return dense

    dense = lax.fori_loop(0, PLANE // batch, step, jnp.zeros((16, samples), F32))
    big = dense.astype(BF16)
    small = (dense - big.astype(F32)).astype(BF16)
    count = FAR * 32
    rows = total_ref[...].astype(BF16).reshape(FAR, NEAR, 32, LOW)
    for near in range(NEAR):
        out_ref[near, :count, :] = rows[:, near].reshape(count, LOW)
        out_ref[near, count : count + 16, :] = big
        out_ref[near, count + 16 : count + 32, :] = small


def merge_near(got_ref, out_ref):
    total = jnp.sum(got_ref[...].astype(F32), axis=0)
    count = FAR * 32
    dense = total[count : count + 16] + total[count + 16 :]
    out_ref[:, 0:32, :] = total[:count].reshape(FAR, 32, LOW).astype(BF16)
    out_ref[:, 32:48, :] = jnp.broadcast_to(dense.astype(BF16)[None], (FAR, 16, LOW))


def merge_far(got_ref, out_ref):
    total = jnp.sum(got_ref[...].astype(F32), axis=0).astype(BF16)
    out_ref[...] = jnp.broadcast_to(total[None], out_ref.shape)


def update_rows(got_ref, table_ref, accum_ref, table_out, accum_out, top_out):
    width = table_ref.shape[1]
    for h in range(4):
        rows = got_ref[:, 8 * h : 8 * h + 8, :].astype(F32).reshape(width, LOW)
        squares = jnp.sum(rows * rows, axis=0, keepdims=True) * (1.0 / width)
        scaled = []
        for half in range(2):
            lanes = slice(128 * half, 128 * half + 128)
            at = slice(2 * h + half, 2 * h + half + 1)
            new_accum = accum_ref[at, :] + squares[:, lanes]
            accum_out[at, :] = new_accum
            scaled.append(rows[:, lanes] * (LEARN_RATE / (jnp.sqrt(new_accum) + ADA_EPS)))
        change = jnp.concatenate(scaled, axis=1).T
        at = slice(h * LOW, (h + 1) * LOW)
        table_out[at, :] = table_ref[at, :] - change
    top_out[:, :LOW] = got_ref[:, 32:40, :].astype(F32).reshape(width, LOW)
    top_out[:, LOW:] = got_ref[:, 40:48, :].astype(F32).reshape(width, LOW)


def exchange(parts, axis, groups=None):
    return lax.all_to_all(
        parts, axis, split_axis=0, concat_axis=0, tiled=True, axis_index_groups=groups
    )


def local(ids, pooled, pre_act, grad_out, w_top, table, accum):
    samples = pooled.shape[0]
    near_groups = [[f * NEAR + n for n in range(NEAR)] for f in range(FAR)]
    far_groups = [[f * NEAR + n for f in range(FAR)] for n in range(NEAR)]
    sent = call(
        local_grads,
        jax.ShapeDtypeStruct((PLANE, 40, samples), BF16),
        (ids.T, pooled, pre_act, grad_out, w_top),
        scratch=[pltpu.VMEM(a.shape, a.dtype) for a in (ids.T, pooled, pre_act, grad_out, w_top)]
        + [pltpu.SemaphoreType.DMA((5,))],
        memory=pl.ANY,
        vmem=64 * 1024 * 1024 - 256 * 1024,
    )
    got = exchange(sent, "replica")
    merged = call(
        merge_rows,
        jax.ShapeDtypeStruct((NEAR, FAR * 32 + 32, LOW), BF16),
        (got,),
        scratch=(
            pltpu.VMEM((TILES * HIGH * COLS, 4 * OWNERS * CAP), BF16),
            pltpu.VMEM((TILES * LOW, 4 * OWNERS * CAP), BF16),
            pltpu.VMEM((TILES * HIGH * COLS, LOW), F32),
        ),
    )
    got = exchange(merged, "shard", near_groups)
    merged = call(merge_near, jax.ShapeDtypeStruct((FAR, 48, LOW), BF16), (got,))
    got = exchange(merged, "shard", far_groups)
    merged = call(merge_far, jax.ShapeDtypeStruct((PLANE, 48, LOW), BF16), (got,))
    got = exchange(merged, "replica")
    rows = table.shape[0]
    new_table, new_accum, grad_top = call(
        update_rows,
        (
            jax.ShapeDtypeStruct(table.shape, F32),
            jax.ShapeDtypeStruct((rows // 128, 128), F32),
            jax.ShapeDtypeStruct(w_top.shape, F32),
        ),
        (got, table, accum.reshape(rows // 128, 128)),
    )
    return (new_table, new_accum.reshape(rows), grad_top)


def solution(mesh):
    return jax.shard_map(
        local,
        mesh=mesh,
        in_specs=(
            P(("shard", "replica"), None),
            P(("shard", "replica"), None),
            P(("shard", "replica"), None),
            P(("shard", "replica"), None),
            P(),
            P("shard", None),
            P("shard"),
        ),
        out_specs=(P("shard", None), P("shard"), P()),
        check_vma=False,
    )
```

```python
import jax
import jax.numpy as jnp
from jax import lax
from jax.experimental import pallas as pl
from jax.experimental.pallas import tpu as pltpu
from jax.sharding import PartitionSpec as P

LEARN_RATE = 0.5
ADA_EPS = 1e-08

BF16 = jnp.bfloat16
F32 = jnp.float32

PLANE = 32
COLS = 8
NEAR = 4
FAR = 8
LOW = 128
HIGH = 16
TILES = 16
OWNERS = 2
CAP = 64
SLOTS = OWNERS * CAP
OWNED = 64
DENSE = 32
BATCH = 8
PAIR = 2
VMEM_BYTES = 40 * 1024 * 1024


def call(body, out_shape, args, scratch=(), memory=pltpu.VMEM, cost=None, vmem=VMEM_BYTES):
    return pl.pallas_call(
        body,
        out_shape=out_shape,
        in_specs=[pl.BlockSpec(memory_space=memory)] * len(args),
        out_specs=jax.tree.map(lambda _: pl.BlockSpec(memory_space=pltpu.VMEM), out_shape),
        scratch_shapes=list(scratch),
        cost_estimate=cost,
        compiler_params=pltpu.CompilerParams(vmem_limit_bytes=vmem),
    )(*args)


def code(number):
    size = (number & 127).astype(F32) * (1.0 / 128.0) + 1.0
    return jnp.where(number >= 128, -size, size)


def slot_tables(ids_ref, samples):
    lookups = ids_ref.shape[0]
    total = lookups * samples
    ids = jnp.concatenate([ids_ref[j : j + 1, :] for j in range(lookups)], axis=1)
    owner = ids // (LOW * HIGH // OWNERS)
    named = (lax.broadcasted_iota(jnp.int32, (PLANE, total), 0) == owner).astype(F32)
    before = (
        lax.broadcasted_iota(jnp.int32, (samples, samples), 0)
        < lax.broadcasted_iota(jnp.int32, (samples, samples), 1)
    ).astype(F32)
    before = before.astype(BF16)
    ranks = []
    carry = jnp.zeros((PLANE, 1), F32)
    for j in range(lookups):
        part = named[:, j * samples : (j + 1) * samples]
        earlier = carry + jnp.dot(part.astype(BF16), before, preferred_element_type=F32)
        ranks.append(jnp.sum(part * earlier, axis=0, keepdims=True))
        carry += jnp.sum(part, axis=1, keepdims=True)
    slot = ((owner % OWNERS) * CAP).astype(F32) + jnp.concatenate(ranks, axis=1)
    place = code(ids % LOW) * (1 << ((ids // LOW) % HIGH)).astype(F32)
    number = code(lax.broadcasted_iota(jnp.int32, (1, total), 1) % samples)
    tile = lax.broadcasted_iota(jnp.int32, (TILES, total), 0) == owner // OWNERS
    tile = tile.astype(F32).astype(BF16)
    at_slot = lax.broadcasted_iota(jnp.int32, (SLOTS, total), 0).astype(F32) == slot
    return [
        lax.dot_general(
            tile,
            jnp.where(at_slot, value, 0.0).astype(BF16),
            (((1,), (1,)), ((), ())),
            preferred_element_type=F32,
        ).astype(BF16)
        for value in (place, number)
    ]


def local_grads(
    ids_hbm, pooled_hbm, pre_hbm, grad_hbm, w_hbm, out_ref, ids_ref, pooled_ref, pre_ref, grad_ref, w_ref, sems
):
    pairs = (
        (ids_hbm, ids_ref),
        (pre_hbm, pre_ref),
        (grad_hbm, grad_ref),
        (w_hbm, w_ref),
        (pooled_hbm, pooled_ref),
    )
    copies = [
        pltpu.make_async_copy(source, target, sems.at[i])
        for i, (source, target) in enumerate(pairs)
    ]
    for copy in copies:
        copy.start()
    copies[0].wait()
    place, number = slot_tables(ids_ref, pooled_ref.shape[0])
    out_ref[:, 32:48, :] = jnp.broadcast_to(place[None], (PLANE, TILES, SLOTS))
    out_ref[:, 48:64, :] = jnp.broadcast_to(number[None], (PLANE, TILES, SLOTS))
    copies[1].wait()
    tanh_pre = jnp.tanh(pre_ref[...].astype(F32))
    copies[2].wait()
    derivative = (grad_ref[...].astype(F32) * (1.0 - tanh_pre * tanh_pre)).astype(BF16)
    copies[3].wait()
    pooled_t = lax.dot_general(
        w_ref[...], derivative, (((1,), (1,)), ((), ())), preferred_element_type=F32
    )
    shape = (PLANE, COLS, LOW)
    out_ref[:, 64:80, :] = jnp.concatenate(
        [pooled_t[:, :LOW].reshape(shape), pooled_t[:, LOW:].reshape(shape)], axis=1
    ).astype(BF16)
    copies[4].wait()
    dense = lax.dot_general(
        pooled_ref[...], derivative, (((0,), (0,)), ((), ())), preferred_element_type=F32
    )
    out_ref[:, 0:32, :] = jnp.concatenate(
        [dense[:, LOW * i : LOW * (i + 1)].reshape(shape) for i in range(4)], axis=1
    ).astype(BF16)


def decode(got_ref, source):
    place = got_ref[source, 32:48, :].astype(F32)
    number = got_ref[source, 48:64, :].astype(F32)
    grad = got_ref[source, 64:80, :].astype(F32)
    lane = jnp.maximum((jnp.abs(number) - 1.0) * 128.0, 0.0).astype(jnp.int32)
    high = jnp.zeros_like(place)
    scale = jnp.ones_like(place)
    for k in range(1, HIGH):
        above = place >= float(1 << k)
        high = jnp.where(above, float(k), high)
        scale = jnp.where(above, 1.0 / (1 << k), scale)
    low = (place * scale - 1.0) * 128.0
    return grad, lane, number < 0.0, place > 0.0, high, low


def merge_rows(got_ref, out_ref, total_ref):
    size = HIGH * COLS
    total_ref[...] = jnp.zeros_like(total_ref)
    second = (lax.broadcasted_iota(jnp.int32, (16, PAIR * SLOTS), 0) >= COLS).astype(F32)
    low_iota = lax.broadcasted_iota(jnp.int32, (LOW, PAIR * SLOTS), 0).astype(F32).astype(BF16)

    def product(tile, members):
        t = slice(tile, tile + 1)
        values, highs, lows = [], [], []
        for grad, lane, upper, filled, high, low in members:
            at = jnp.broadcast_to(lane[t], (COLS, SLOTS))
            value = jnp.where(
                upper[t],
                jnp.take_along_axis(grad[COLS:], at, axis=1),
                jnp.take_along_axis(grad[:COLS], at, axis=1),
            )
            values.append(jnp.where(filled[t], value, 0.0))
            highs.append(high[t])
            lows.append(low[t])
        value = jnp.concatenate(values, axis=1)
        value = jnp.concatenate([value, value], axis=0).astype(BF16)
        which = jnp.broadcast_to(jnp.concatenate(highs, axis=1), value.shape) - second
        which = which.astype(BF16)
        at_high = jnp.concatenate(
            [
                jnp.where(which == jnp.asarray(2 * k, BF16), value, jnp.zeros_like(value))
                for k in range(HIGH // 2)
            ],
            axis=0,
        )
        digit = jnp.broadcast_to(jnp.concatenate(lows, axis=1), low_iota.shape).astype(BF16)
        at_low = jnp.where(digit == low_iota, jnp.ones_like(digit), jnp.zeros_like(digit))
        return lax.dot_general(
            at_high, at_low, (((1,), (1,)), ((), ())), preferred_element_type=F32
        )

    def step(index, dense):
        pairs = []
        for pair in range(BATCH // PAIR):
            sources = [index * BATCH + pair * PAIR + member for member in range(PAIR)]
            pairs.append([decode(got_ref, source) for source in sources])
            for source in sources:
                dense += got_ref[source, 0:32, :].astype(F32)
        for tile in range(TILES):
            rows = slice(size * tile, size * (tile + 1))
            total = product(tile, pairs[0])
            for members in pairs[1:]:
                total += product(tile, members)
            total_ref[rows, :] += total
        return dense

    dense = lax.fori_loop(0, PLANE // BATCH, step, jnp.zeros((DENSE, LOW), F32))
    big = dense.astype(BF16)
    small = (dense - big.astype(F32)).astype(BF16)
    count = FAR * OWNED
    rows = total_ref[...].astype(BF16).reshape(FAR, NEAR, OWNED, LOW)
    for near in range(NEAR):
        out_ref[near, :count, :] = rows[:, near].reshape(count, LOW)
        out_ref[near, count : count + DENSE, :] = big
        out_ref[near, count + DENSE :, :] = small


def merge_near(got_ref, out_ref):
    total = jnp.sum(got_ref[...].astype(F32), axis=0)
    count = FAR * OWNED
    dense = total[count : count + DENSE] + total[count + DENSE :]
    out_ref[:, :OWNED, :] = total[:count].reshape(FAR, OWNED, LOW).astype(BF16)
    out_ref[:, OWNED:, :] = jnp.broadcast_to(dense.astype(BF16)[None], (FAR, DENSE, LOW))


def merge_far(got_ref, out_ref):
    total = jnp.sum(got_ref[...].astype(F32), axis=0).astype(BF16)
    out_ref[...] = jnp.broadcast_to(total[None], out_ref.shape)


def update_rows(got_ref, table_ref, accum_ref, table_out, accum_out, top_out):
    width = table_ref.shape[1]
    for h in range(OWNED // COLS):
        rows = got_ref[:, COLS * h : COLS * (h + 1), :].astype(F32).reshape(width, LOW)
        squares = jnp.sum(rows * rows, axis=0, keepdims=True) * (1.0 / width)
        new_accum = accum_ref[h : h + 1, :] + squares
        accum_out[h : h + 1, :] = new_accum
        change = (rows * (LEARN_RATE / (jnp.sqrt(new_accum) + ADA_EPS))).T
        at = slice(h * LOW, (h + 1) * LOW)
        table_out[at, :] = table_ref[at, :] - change
    for i in range(4):
        first = OWNED + COLS * i
        top_out[:, LOW * i : LOW * (i + 1)] = (
            got_ref[:, first : first + COLS, :].astype(F32).reshape(width, LOW)
        )


def exchange(parts, axis, groups=None):
    return lax.all_to_all(
        parts, axis, split_axis=0, concat_axis=0, tiled=True, axis_index_groups=groups
    )


def local(ids, pooled, pre_act, grad_out, w_top, table, accum):
    near_groups = [[f * NEAR + n for n in range(NEAR)] for f in range(FAR)]
    far_groups = [[f * NEAR + n for f in range(FAR)] for n in range(NEAR)]
    inputs = (ids.T, pooled, pre_act, grad_out, w_top)
    sent = call(
        local_grads,
        jax.ShapeDtypeStruct((PLANE, 80, LOW), BF16),
        inputs,
        scratch=[pltpu.VMEM(a.shape, a.dtype) for a in inputs]
        + [pltpu.SemaphoreType.DMA((5,))],
        memory=pl.ANY,
        vmem=64 * 1024 * 1024 - 256 * 1024,
    )
    got = exchange(sent, "replica")
    merged = call(
        merge_rows,
        jax.ShapeDtypeStruct((NEAR, FAR * OWNED + 2 * DENSE, LOW), BF16),
        (got,),
        scratch=(
            pltpu.VMEM((TILES * HIGH * COLS, LOW), F32),
        ),
    )
    got = exchange(merged, "shard", near_groups)
    merged = call(merge_near, jax.ShapeDtypeStruct((FAR, OWNED + DENSE, LOW), BF16), (got,))
    got = exchange(merged, "shard", far_groups)
    merged = call(merge_far, jax.ShapeDtypeStruct((PLANE, OWNED + DENSE, LOW), BF16), (got,))
    got = exchange(merged, "replica")
    rows = table.shape[0]
    new_table, new_accum, grad_top = call(
        update_rows,
        (
            jax.ShapeDtypeStruct(table.shape, F32),
            jax.ShapeDtypeStruct((rows // 128, 128), F32),
            jax.ShapeDtypeStruct(w_top.shape, F32),
        ),
        (got, table, accum.reshape(rows // 128, 128)),
    )
    return (new_table, new_accum.reshape(rows), grad_top)


def solution(mesh):
    return jax.shard_map(
        local,
        mesh=mesh,
        in_specs=(
            P(("shard", "replica"), None),
            P(("shard", "replica"), None),
            P(("shard", "replica"), None),
            P(("shard", "replica"), None),
            P(),
            P("shard", None),
            P("shard"),
        ),
        out_specs=(P("shard", None), P("shard"), P()),
        check_vma=False,
    )
```

```python
import jax
import jax.numpy as jnp
from jax import lax
from jax.experimental import pallas as pl
from jax.experimental.pallas import tpu as pltpu
from jax.sharding import PartitionSpec as P

LEARN_RATE = 0.5
ADA_EPS = 1e-08

BF16 = jnp.bfloat16
F32 = jnp.float32

PLANE = 32
COLS = 8
CORES = 2
NEAR = 4
FAR = 8
LOW = 128
HIGH = 16
TILES = 16
OWNERS = 2
CAP = 64
SLOTS = OWNERS * CAP
OWNED = 64
DENSE = 32
BATCH = 8
PAIR = 2
VMEM_BYTES = 40 * 1024 * 1024


def call(body, out_shape, args, scratch=(), memory=pltpu.VMEM, cost=None, vmem=VMEM_BYTES):
    return pl.pallas_call(
        body,
        out_shape=out_shape,
        in_specs=[pl.BlockSpec(memory_space=memory)] * len(args),
        out_specs=jax.tree.map(lambda _: pl.BlockSpec(memory_space=pltpu.VMEM), out_shape),
        scratch_shapes=list(scratch),
        cost_estimate=cost,
        compiler_params=pltpu.CompilerParams(vmem_limit_bytes=vmem),
    )(*args)


def code(number):
    size = (number & 127).astype(F32) * (1.0 / 128.0) + 1.0
    return jnp.where(number >= 128, -size, size)


def slot_tables(ids_ref, samples):
    lookups = ids_ref.shape[0]
    total = lookups * samples
    ids = jnp.concatenate([ids_ref[j : j + 1, :] for j in range(lookups)], axis=1)
    owner = ids // (LOW * HIGH // OWNERS)
    named = (lax.broadcasted_iota(jnp.int32, (PLANE, total), 0) == owner).astype(F32)
    before = (
        lax.broadcasted_iota(jnp.int32, (samples, samples), 0)
        < lax.broadcasted_iota(jnp.int32, (samples, samples), 1)
    ).astype(F32)
    before = before.astype(BF16)
    ranks = []
    carry = jnp.zeros((PLANE, 1), F32)
    for j in range(lookups):
        part = named[:, j * samples : (j + 1) * samples]
        earlier = carry + jnp.dot(part.astype(BF16), before, preferred_element_type=F32)
        ranks.append(jnp.sum(part * earlier, axis=0, keepdims=True))
        carry += jnp.sum(part, axis=1, keepdims=True)
    slot = ((owner % OWNERS) * CAP).astype(F32) + jnp.concatenate(ranks, axis=1)
    place = code(ids % LOW) * (1 << ((ids // LOW) % HIGH)).astype(F32)
    number = code(lax.broadcasted_iota(jnp.int32, (1, total), 1) % samples)
    tile = owner // OWNERS
    kinds = [(tile + TILES - core) % TILES for core in range(CORES)]
    kinds = [kind ^ (kind // (TILES // 2)) for kind in kinds]
    tile = jnp.concatenate(
        [lax.broadcasted_iota(jnp.int32, (TILES, total), 0) == kind for kind in kinds], axis=0
    )
    tile = tile.astype(F32).astype(BF16)
    at_slot = lax.broadcasted_iota(jnp.int32, (SLOTS, total), 0).astype(F32) == slot
    return [
        lax.dot_general(
            tile,
            jnp.where(at_slot, value, 0.0).astype(BF16),
            (((1,), (1,)), ((), ())),
            preferred_element_type=F32,
        ).astype(BF16).reshape(1, CORES, TILES, SLOTS)
        for value in (place, number)
    ]


def local_grads(
    ids_hbm, pooled_hbm, pre_hbm, grad_hbm, w_hbm, out_ref, ids_ref, pooled_ref, pre_ref, grad_ref, w_ref, sems
):
    pairs = (
        (ids_hbm, ids_ref),
        (pre_hbm, pre_ref),
        (grad_hbm, grad_ref),
        (w_hbm, w_ref),
        (pooled_hbm, pooled_ref),
    )
    copies = [
        pltpu.make_async_copy(source, target, sems.at[i])
        for i, (source, target) in enumerate(pairs)
    ]
    for copy in copies:
        copy.start()
    copies[0].wait()
    place, number = slot_tables(ids_ref, pooled_ref.shape[0])
    shape = (PLANE // CORES, CORES, TILES, SLOTS)
    out_ref[:, 32:48, :] = jnp.broadcast_to(place, shape).reshape(PLANE, TILES, SLOTS)
    out_ref[:, 48:64, :] = jnp.broadcast_to(number, shape).reshape(PLANE, TILES, SLOTS)
    copies[1].wait()
    tanh_pre = jnp.tanh(pre_ref[...].astype(F32))
    copies[2].wait()
    derivative = (grad_ref[...].astype(F32) * (1.0 - tanh_pre * tanh_pre)).astype(BF16)
    copies[3].wait()
    pooled_t = lax.dot_general(
        w_ref[...], derivative, (((1,), (1,)), ((), ())), preferred_element_type=F32
    )
    shape = (PLANE, COLS, LOW)
    out_ref[:, 64:80, :] = jnp.concatenate(
        [pooled_t[:, :LOW].reshape(shape), pooled_t[:, LOW:].reshape(shape)], axis=1
    ).astype(BF16)
    copies[4].wait()
    dense = lax.dot_general(
        pooled_ref[...], derivative, (((0,), (0,)), ((), ())), preferred_element_type=F32
    )
    out_ref[:, 0:32, :] = jnp.concatenate(
        [dense[:, LOW * i : LOW * (i + 1)].reshape(shape) for i in range(4)], axis=1
    ).astype(BF16)


def decode(got_ref, source):
    place = got_ref[source, 32:48, :].astype(F32)
    number = got_ref[source, 48:64, :].astype(F32)
    grad = got_ref[source, 64:80, :].astype(F32)
    lane = jnp.maximum((jnp.abs(number) - 1.0) * 128.0, 0.0).astype(jnp.int32)
    high = jnp.zeros_like(place)
    scale = jnp.ones_like(place)
    for k in range(1, HIGH):
        above = place >= float(1 << k)
        high = jnp.where(above, float(k), high)
        scale = jnp.where(above, 1.0 / (1 << k), scale)
    low = (place * scale - 1.0) * 128.0
    return grad, lane, number < 0.0, place > 0.0, high, low


def merge_rows(got_ref, out_ref, total_ref):
    size = HIGH * COLS
    total_ref[...] = jnp.zeros_like(total_ref)
    second = (lax.broadcasted_iota(jnp.int32, (16, PAIR * SLOTS), 0) >= COLS).astype(F32)
    low_iota = lax.broadcasted_iota(jnp.int32, (LOW, PAIR * SLOTS), 0).astype(F32).astype(BF16)

    def product(tile, members):
        t = slice(tile, tile + 1)
        values, highs, lows = [], [], []
        for grad, lane, upper, filled, high, low in members:
            at = jnp.broadcast_to(lane[t], (COLS, SLOTS))
            value = jnp.where(
                upper[t],
                jnp.take_along_axis(grad[COLS:], at, axis=1),
                jnp.take_along_axis(grad[:COLS], at, axis=1),
            )
            values.append(jnp.where(filled[t], value, 0.0))
            highs.append(high[t])
            lows.append(low[t])
        value = jnp.concatenate(values, axis=1)
        value = jnp.concatenate([value, value], axis=0).astype(BF16)
        which = jnp.broadcast_to(jnp.concatenate(highs, axis=1), value.shape) - second
        which = which.astype(BF16)
        at_high = jnp.concatenate(
            [
                jnp.where(which == jnp.asarray(2 * k, BF16), value, jnp.zeros_like(value))
                for k in range(HIGH // 2)
            ],
            axis=0,
        )
        digit = jnp.broadcast_to(jnp.concatenate(lows, axis=1), low_iota.shape).astype(BF16)
        at_low = jnp.where(digit == low_iota, jnp.ones_like(digit), jnp.zeros_like(digit))
        return lax.dot_general(
            at_high, at_low, (((1,), (1,)), ((), ())), preferred_element_type=F32
        )

    def step(index, dense):
        pairs = []
        for pair in range(BATCH // PAIR):
            sources = [index * BATCH + pair * PAIR + member for member in range(PAIR)]
            pairs.append([decode(got_ref, source) for source in sources])
            for source in sources:
                dense += got_ref[source, 0:32, :].astype(F32)
        for tile in range(TILES):
            rows = slice(size * tile, size * (tile + 1))
            total = product(tile, pairs[0])
            for members in pairs[1:]:
                total += product(tile, members)
            total_ref[rows, :] += total
        return dense

    dense = lax.fori_loop(0, PLANE // BATCH, step, jnp.zeros((DENSE, LOW), F32))
    big = dense.astype(BF16)
    small = (dense - big.astype(F32)).astype(BF16)
    count = FAR * OWNED
    rows = total_ref[...].astype(BF16).reshape(FAR, NEAR, OWNED, LOW)
    for near in range(NEAR):
        out_ref[near, :count, :] = rows[:, near].reshape(count, LOW)
        out_ref[near, count : count + DENSE, :] = big
        out_ref[near, count + DENSE :, :] = small


def merge_near(got_ref, out_ref):
    total = jnp.sum(got_ref[...].astype(F32), axis=0)
    count = FAR * OWNED
    dense = total[count : count + DENSE] + total[count + DENSE :]
    out_ref[:, :OWNED, :] = total[:count].reshape(FAR, OWNED, LOW).astype(BF16)
    out_ref[:, OWNED:, :] = jnp.broadcast_to(dense.astype(BF16)[None], (FAR, DENSE, LOW))


def merge_far(got_ref, out_ref):
    total = jnp.sum(got_ref[...].astype(F32), axis=0).astype(BF16)
    out_ref[...] = jnp.broadcast_to(total[None], out_ref.shape)


def update_rows(got_ref, table_ref, accum_ref, table_out, accum_out, top_out):
    width = table_ref.shape[1]
    for h in range(OWNED // COLS):
        rows = got_ref[:, COLS * h : COLS * (h + 1), :].astype(F32).reshape(width, LOW)
        squares = jnp.sum(rows * rows, axis=0, keepdims=True) * (1.0 / width)
        new_accum = accum_ref[h : h + 1, :] + squares
        accum_out[h : h + 1, :] = new_accum
        change = (rows * (LEARN_RATE / (jnp.sqrt(new_accum) + ADA_EPS))).T
        at = slice(h * LOW, (h + 1) * LOW)
        table_out[at, :] = table_ref[at, :] - change
    for i in range(4):
        first = OWNED + COLS * i
        top_out[:, LOW * i : LOW * (i + 1)] = (
            got_ref[:, first : first + COLS, :].astype(F32).reshape(width, LOW)
        )


def plane_of(far, near, core):
    turned = (near + 2 * (far >= FAR // 2)) % NEAR
    return (far * NEAR + turned + 2 * core) % (FAR * NEAR)


def exchange(parts, axis, groups=None):
    return lax.all_to_all(
        parts, axis, split_axis=0, concat_axis=0, tiled=True, axis_index_groups=groups
    )


def local(ids, pooled, pre_act, grad_out, w_top, table, accum):
    both = ("shard", "replica")

    def place_of(far, near, member):
        return plane_of(far, near, member % CORES) * PLANE + member

    near_groups = [
        [place_of(f, n, member) for n in range(NEAR)] for member in range(PLANE) for f in range(FAR)
    ]
    far_groups = [
        [place_of(f, n, member) for f in range(FAR)] for member in range(PLANE) for n in range(NEAR)
    ]
    inputs = (ids.T, pooled, pre_act, grad_out, w_top)
    sent = call(
        local_grads,
        jax.ShapeDtypeStruct((PLANE, 80, LOW), BF16),
        inputs,
        scratch=[pltpu.VMEM(a.shape, a.dtype) for a in inputs]
        + [pltpu.SemaphoreType.DMA((5,))],
        memory=pl.ANY,
        vmem=64 * 1024 * 1024 - 256 * 1024,
    )
    got = exchange(sent, "replica")
    merged = call(
        merge_rows,
        jax.ShapeDtypeStruct((NEAR, FAR * OWNED + 2 * DENSE, LOW), BF16),
        (got,),
        scratch=(
            pltpu.VMEM((TILES * HIGH * COLS, LOW), F32),
        ),
    )
    got = exchange(merged, both, near_groups)
    merged = call(merge_near, jax.ShapeDtypeStruct((FAR, OWNED + DENSE, LOW), BF16), (got,))
    got = exchange(merged, both, far_groups)
    merged = call(merge_far, jax.ShapeDtypeStruct((PLANE, OWNED + DENSE, LOW), BF16), (got,))
    got = exchange(merged, "replica")
    rows = table.shape[0]
    new_table, new_accum, grad_top = call(
        update_rows,
        (
            jax.ShapeDtypeStruct(table.shape, F32),
            jax.ShapeDtypeStruct((rows // 128, 128), F32),
            jax.ShapeDtypeStruct(w_top.shape, F32),
        ),
        (got, table, accum.reshape(rows // 128, 128)),
    )
    return (new_table, new_accum.reshape(rows), grad_top)


def solution(mesh):
    return jax.shard_map(
        local,
        mesh=mesh,
        in_specs=(
            P(("shard", "replica"), None),
            P(("shard", "replica"), None),
            P(("shard", "replica"), None),
            P(("shard", "replica"), None),
            P(),
            P("shard", None),
            P("shard"),
        ),
        out_specs=(P("shard", None), P("shard"), P()),
        check_vma=False,
    )
```

```python
import jax
import jax.numpy as jnp
from jax import lax
from jax.experimental import pallas as pl
from jax.experimental.pallas import tpu as pltpu
from jax.sharding import PartitionSpec as P

LEARN_RATE = 0.5
ADA_EPS = 1e-08

BF16 = jnp.bfloat16
F32 = jnp.float32

PLANE = 32
COLS = 8
CORES = 2
NEAR = 4
FAR = 8
LOW = 128
HIGH = 16
TILES = 16
OWNERS = 2
CAP = 64
SLOTS = OWNERS * CAP
OWNED = 64
DENSE = 32
BATCH = 8
PAIR = 2
VMEM_BYTES = 40 * 1024 * 1024


def call(body, out_shape, args, scratch=(), memory=pltpu.VMEM, direct=(), vmem=VMEM_BYTES):
    return pl.pallas_call(
        body,
        out_shape=out_shape,
        in_specs=[pl.BlockSpec(memory_space=memory)] * len(args),
        out_specs=jax.tree.unflatten(
            jax.tree.structure(out_shape),
            [
                pl.BlockSpec(memory_space=pl.ANY if i in direct else pltpu.VMEM)
                for i in range(len(jax.tree.leaves(out_shape)))
            ],
        ),
        scratch_shapes=list(scratch),
        compiler_params=pltpu.CompilerParams(vmem_limit_bytes=vmem),
    )(*args)


def code(number):
    size = (number & 127).astype(F32) * (1.0 / 128.0) + 1.0
    return jnp.where(number >= 128, -size, size)


def slot_tables(ids_ref, samples):
    lookups = ids_ref.shape[0]
    total = lookups * samples
    ids = jnp.concatenate([ids_ref[j : j + 1, :] for j in range(lookups)], axis=1)
    owner = ids // (LOW * HIGH // OWNERS)
    named = (lax.broadcasted_iota(jnp.int32, (PLANE, total), 0) == owner).astype(F32)
    before = (
        lax.broadcasted_iota(jnp.int32, (samples, samples), 0)
        < lax.broadcasted_iota(jnp.int32, (samples, samples), 1)
    ).astype(F32)
    before = before.astype(BF16)
    ranks = []
    carry = jnp.zeros((PLANE, 1), F32)
    for j in range(lookups):
        part = named[:, j * samples : (j + 1) * samples]
        earlier = carry + jnp.dot(part.astype(BF16), before, preferred_element_type=F32)
        ranks.append(jnp.sum(part * earlier, axis=0, keepdims=True))
        carry += jnp.sum(part, axis=1, keepdims=True)
    slot = ((owner % OWNERS) * CAP).astype(F32) + jnp.concatenate(ranks, axis=1)
    place = code(ids % LOW) * (1 << ((ids // LOW) % HIGH)).astype(F32)
    number = code(lax.broadcasted_iota(jnp.int32, (1, total), 1) % samples)
    tile = owner // OWNERS
    kinds = [(tile + TILES - core) % TILES for core in range(CORES)]
    kinds = [kind ^ (kind // (TILES // 2)) for kind in kinds]
    tile = jnp.concatenate(
        [lax.broadcasted_iota(jnp.int32, (TILES, total), 0) == kind for kind in kinds], axis=0
    )
    tile = tile.astype(F32).astype(BF16)
    at_slot = lax.broadcasted_iota(jnp.int32, (SLOTS, total), 0).astype(F32) == slot
    return [
        lax.dot_general(
            tile,
            jnp.where(at_slot, value, 0.0).astype(BF16),
            (((1,), (1,)), ((), ())),
            preferred_element_type=F32,
        ).astype(BF16).reshape(1, CORES, TILES, SLOTS)
        for value in (place, number)
    ]


def local_grads(
    ids_hbm, pooled_hbm, pre_hbm, grad_hbm, w_hbm, out_ref, ids_ref, pooled_ref, pre_ref, grad_ref, w_ref, sems
):
    pairs = (
        (ids_hbm, ids_ref),
        (pre_hbm, pre_ref),
        (grad_hbm, grad_ref),
        (w_hbm, w_ref),
        (pooled_hbm, pooled_ref),
    )
    copies = [
        pltpu.make_async_copy(source, target, sems.at[i])
        for i, (source, target) in enumerate(pairs)
    ]
    for copy in copies:
        copy.start()
    copies[0].wait()
    place, number = slot_tables(ids_ref, pooled_ref.shape[0])
    shape = (PLANE // CORES, CORES, TILES, SLOTS)
    out_ref[:, 32:48, :] = jnp.broadcast_to(place, shape).reshape(PLANE, TILES, SLOTS)
    out_ref[:, 48:64, :] = jnp.broadcast_to(number, shape).reshape(PLANE, TILES, SLOTS)
    copies[1].wait()
    tanh_pre = jnp.tanh(pre_ref[...].astype(F32))
    copies[2].wait()
    derivative = (grad_ref[...].astype(F32) * (1.0 - tanh_pre * tanh_pre)).astype(BF16)
    copies[3].wait()
    pooled_t = lax.dot_general(
        w_ref[...], derivative, (((1,), (1,)), ((), ())), preferred_element_type=F32
    )
    shape = (PLANE, COLS, LOW)
    out_ref[:, 64:80, :] = jnp.concatenate(
        [pooled_t[:, :LOW].reshape(shape), pooled_t[:, LOW:].reshape(shape)], axis=1
    ).astype(BF16)
    copies[4].wait()
    dense = lax.dot_general(
        pooled_ref[...], derivative, (((0,), (0,)), ((), ())), preferred_element_type=F32
    )
    out_ref[:, 0:32, :] = jnp.concatenate(
        [dense[:, LOW * i : LOW * (i + 1)].reshape(shape) for i in range(4)], axis=1
    ).astype(BF16)


def decode(got_ref, source):
    place = got_ref[source, 32:48, :].astype(F32)
    number = got_ref[source, 48:64, :].astype(F32)
    grad = got_ref[source, 64:80, :].astype(F32)
    lane = jnp.maximum((jnp.abs(number) - 1.0) * 128.0, 0.0).astype(jnp.int32)
    high = jnp.zeros_like(place)
    scale = jnp.ones_like(place)
    for k in range(1, HIGH):
        above = place >= float(1 << k)
        high = jnp.where(above, float(k), high)
        scale = jnp.where(above, 1.0 / (1 << k), scale)
    low = (place * scale - 1.0) * 128.0
    return grad, lane, number < 0.0, place > 0.0, high, low


def merge_rows(got_ref, out_ref, total_ref):
    size = HIGH * COLS
    total_ref[...] = jnp.zeros_like(total_ref)
    second = (lax.broadcasted_iota(jnp.int32, (16, PAIR * SLOTS), 0) >= COLS).astype(F32)
    low_iota = lax.broadcasted_iota(jnp.int32, (LOW, PAIR * SLOTS), 0).astype(F32).astype(BF16)

    def product(tile, members):
        t = slice(tile, tile + 1)
        values, highs, lows = [], [], []
        for grad, lane, upper, filled, high, low in members:
            at = jnp.broadcast_to(lane[t], (COLS, SLOTS))
            value = jnp.where(
                upper[t],
                jnp.take_along_axis(grad[COLS:], at, axis=1),
                jnp.take_along_axis(grad[:COLS], at, axis=1),
            )
            values.append(jnp.where(filled[t], value, 0.0))
            highs.append(high[t])
            lows.append(low[t])
        value = jnp.concatenate(values, axis=1)
        value = jnp.concatenate([value, value], axis=0).astype(BF16)
        which = jnp.broadcast_to(jnp.concatenate(highs, axis=1), value.shape) - second
        which = which.astype(BF16)
        at_high = jnp.concatenate(
            [
                jnp.where(which == jnp.asarray(2 * k, BF16), value, jnp.zeros_like(value))
                for k in range(HIGH // 2)
            ],
            axis=0,
        )
        digit = jnp.broadcast_to(jnp.concatenate(lows, axis=1), low_iota.shape).astype(BF16)
        at_low = jnp.where(digit == low_iota, jnp.ones_like(digit), jnp.zeros_like(digit))
        return lax.dot_general(
            at_high, at_low, (((1,), (1,)), ((), ())), preferred_element_type=F32
        )

    def step(index, dense):
        pairs = []
        for pair in range(BATCH // PAIR):
            sources = [index * BATCH + pair * PAIR + member for member in range(PAIR)]
            pairs.append([decode(got_ref, source) for source in sources])
            for source in sources:
                dense += got_ref[source, 0:32, :].astype(F32)
        for tile in range(TILES):
            rows = slice(size * tile, size * (tile + 1))
            total = product(tile, pairs[0])
            for members in pairs[1:]:
                total += product(tile, members)
            total_ref[rows, :] += total
        return dense

    dense = lax.fori_loop(0, PLANE // BATCH, step, jnp.zeros((DENSE, LOW), F32))
    big = dense.astype(BF16)
    small = (dense - big.astype(F32)).astype(BF16)
    count = FAR * OWNED
    rows = total_ref[...].astype(BF16).reshape(FAR, NEAR, OWNED, LOW)
    for near in range(NEAR):
        out_ref[near, :count, :] = rows[:, near].reshape(count, LOW)
        out_ref[near, count : count + DENSE, :] = big
        out_ref[near, count + DENSE :, :] = small


def merge_near(got_ref, out_ref):
    total = jnp.sum(got_ref[...].astype(F32), axis=0)
    count = FAR * OWNED
    dense = total[count : count + DENSE] + total[count + DENSE :]
    out_ref[:, :OWNED, :] = total[:count].reshape(FAR, OWNED, LOW).astype(BF16)
    out_ref[:, OWNED:, :] = jnp.broadcast_to(dense.astype(BF16)[None], (FAR, DENSE, LOW))


def merge_far(got_ref, out_ref):
    total = jnp.sum(got_ref[...].astype(F32), axis=0).astype(BF16)
    out_ref[...] = jnp.broadcast_to(total[None], out_ref.shape)


def update_rows(
    got_ref, table_ref, accum_ref, table_hbm, accum_out, top_hbm, table_out, top_out, sems
):
    width = table_ref.shape[1]
    for i in range(4):
        first = OWNED + COLS * i
        top_out[:, LOW * i : LOW * (i + 1)] = (
            got_ref[:, first : first + COLS, :].astype(F32).reshape(width, LOW)
        )
    copies = [pltpu.make_async_copy(top_out, top_hbm, sems.at[0])]
    copies[0].start()
    for h in range(OWNED // COLS):
        rows = got_ref[:, COLS * h : COLS * (h + 1), :].astype(F32).reshape(width, LOW)
        squares = jnp.sum(rows * rows, axis=0, keepdims=True) * (1.0 / width)
        new_accum = accum_ref[h : h + 1, :] + squares
        accum_out[h : h + 1, :] = new_accum
        change = (rows * (LEARN_RATE / (jnp.sqrt(new_accum) + ADA_EPS))).T
        at = slice(h * LOW, (h + 1) * LOW)
        table_out[at, :] = table_ref[at, :] - change
        copies.append(
            pltpu.make_async_copy(table_out.at[at, :], table_hbm.at[at, :], sems.at[h + 1])
        )
        copies[-1].start()
    for copy in copies:
        copy.wait()


def plane_of(far, near, core):
    turned = (near + 2 * (far >= FAR // 2)) % NEAR
    return (far * NEAR + turned + 2 * core) % (FAR * NEAR)


def exchange(parts, axis, groups=None):
    return lax.all_to_all(
        parts, axis, split_axis=0, concat_axis=0, tiled=True, axis_index_groups=groups
    )


def local(ids, pooled, pre_act, grad_out, w_top, table, accum):
    both = ("shard", "replica")

    def place_of(far, near, member):
        return plane_of(far, near, member % CORES) * PLANE + member

    near_groups = [
        [place_of(f, n, member) for n in range(NEAR)] for member in range(PLANE) for f in range(FAR)
    ]
    far_groups = [
        [place_of(f, n, member) for f in range(FAR)] for member in range(PLANE) for n in range(NEAR)
    ]
    inputs = (ids.T, pooled, pre_act, grad_out, w_top)
    sent = call(
        local_grads,
        jax.ShapeDtypeStruct((PLANE, 80, LOW), BF16),
        inputs,
        scratch=[pltpu.VMEM(a.shape, a.dtype) for a in inputs]
        + [pltpu.SemaphoreType.DMA((5,))],
        memory=pl.ANY,
        vmem=64 * 1024 * 1024 - 256 * 1024,
    )
    got = exchange(sent, "replica")
    merged = call(
        merge_rows,
        jax.ShapeDtypeStruct((NEAR, FAR * OWNED + 2 * DENSE, LOW), BF16),
        (got,),
        scratch=(
            pltpu.VMEM((TILES * HIGH * COLS, LOW), F32),
        ),
    )
    got = exchange(merged, both, near_groups)
    merged = call(merge_near, jax.ShapeDtypeStruct((FAR, OWNED + DENSE, LOW), BF16), (got,))
    got = exchange(merged, both, far_groups)
    merged = call(merge_far, jax.ShapeDtypeStruct((PLANE, OWNED + DENSE, LOW), BF16), (got,))
    got = exchange(merged, "replica")
    rows = table.shape[0]
    new_table, new_accum, grad_top = call(
        update_rows,
        (
            jax.ShapeDtypeStruct(table.shape, F32),
            jax.ShapeDtypeStruct((rows // 128, 128), F32),
            jax.ShapeDtypeStruct(w_top.shape, F32),
        ),
        (got, table, accum.reshape(rows // 128, 128)),
        scratch=(
            pltpu.VMEM(table.shape, F32),
            pltpu.VMEM(w_top.shape, F32),
            pltpu.SemaphoreType.DMA((OWNED // COLS + 1,)),
        ),
        direct=(0, 2),
    )
    return (new_table, new_accum.reshape(rows), grad_top)


def solution(mesh):
    return jax.shard_map(
        local,
        mesh=mesh,
        in_specs=(
            P(("shard", "replica"), None),
            P(("shard", "replica"), None),
            P(("shard", "replica"), None),
            P(("shard", "replica"), None),
            P(),
            P("shard", None),
            P("shard"),
        ),
        out_specs=(P("shard", None), P("shard"), P()),
        check_vma=False,
    )
```

```python
import jax
import jax.numpy as jnp
from jax import lax
from jax.experimental import pallas as pl
from jax.experimental.pallas import tpu as pltpu
from jax.sharding import PartitionSpec as P

LEARN_RATE = 0.5
ADA_EPS = 1e-08

BF16 = jnp.bfloat16
F32 = jnp.float32

PLANE = 32
COLS = 8
CORES = 2
NEAR = 4
FAR = 8
LOW = 128
HIGH = 16
TILES = 16
OWNERS = 2
CAP = 64
SLOTS = OWNERS * CAP
OWNED = 64
DENSE = 32
BATCH = 8
PAIR = 2
FAR_ORDER = (0, 4, 7, 3, 6, 2, 5, 1)
PLANE_ORDER = tuple(5 * k % PLANE for k in range(PLANE))
VMEM_BYTES = 40 * 1024 * 1024


def call(body, out_shape, args, scratch=(), memory=pltpu.VMEM, cost=None, vmem=VMEM_BYTES):
    return pl.pallas_call(
        body,
        out_shape=out_shape,
        in_specs=[pl.BlockSpec(memory_space=memory)] * len(args),
        out_specs=jax.tree.map(lambda _: pl.BlockSpec(memory_space=pltpu.VMEM), out_shape),
        scratch_shapes=list(scratch),
        cost_estimate=cost,
        compiler_params=pltpu.CompilerParams(vmem_limit_bytes=vmem),
    )(*args)


def code(number):
    size = (number & 127).astype(F32) * (1.0 / 128.0) + 1.0
    return jnp.where(number >= 128, -size, size)


def by_member(columns):
    blocks = [columns[COLS * p : COLS * (p + 1)] for p in PLANE_ORDER]
    return jnp.concatenate(blocks, axis=0).reshape(PLANE, COLS, LOW)


def from_members(got_ref, first):
    blocks = [
        got_ref[PLANE_ORDER.index(p), first : first + COLS, :].astype(F32) for p in range(PLANE)
    ]
    return jnp.concatenate(blocks, axis=0)


def slot_tables(ids_ref, samples):
    lookups = ids_ref.shape[0]
    total = lookups * samples
    ids = jnp.concatenate([ids_ref[j : j + 1, :] for j in range(lookups)], axis=1)
    owner = ids // (LOW * HIGH // OWNERS)
    named = (lax.broadcasted_iota(jnp.int32, (PLANE, total), 0) == owner).astype(F32)
    before = (
        lax.broadcasted_iota(jnp.int32, (samples, samples), 0)
        < lax.broadcasted_iota(jnp.int32, (samples, samples), 1)
    ).astype(F32)
    before = before.astype(BF16)
    ranks = []
    carry = jnp.zeros((PLANE, 1), F32)
    for j in range(lookups):
        part = named[:, j * samples : (j + 1) * samples]
        earlier = carry + jnp.dot(part.astype(BF16), before, preferred_element_type=F32)
        ranks.append(jnp.sum(part * earlier, axis=0, keepdims=True))
        carry += jnp.sum(part, axis=1, keepdims=True)
    slot = ((owner % OWNERS) * CAP).astype(F32) + jnp.concatenate(ranks, axis=1)
    place = code(ids % LOW) * (1 << ((ids // LOW) % HIGH)).astype(F32)
    number = code(lax.broadcasted_iota(jnp.int32, (1, total), 1) % samples)
    tile = owner // OWNERS
    kinds = [(tile + TILES - core) % TILES for core in range(CORES)]
    kinds = [kind ^ (kind // (TILES // 2)) for kind in kinds]
    kinds = [
        sum(jnp.where(kind // 2 == group, 2 * k, 0) for k, group in enumerate(FAR_ORDER))
        + kind % 2
        for kind in kinds
    ]
    tile = jnp.concatenate(
        [lax.broadcasted_iota(jnp.int32, (TILES, total), 0) == kind for kind in kinds], axis=0
    )
    tile = tile.astype(F32).astype(BF16)
    at_slot = lax.broadcasted_iota(jnp.int32, (SLOTS, total), 0).astype(F32) == slot
    return [
        lax.dot_general(
            tile,
            jnp.where(at_slot, value, 0.0).astype(BF16),
            (((1,), (1,)), ((), ())),
            preferred_element_type=F32,
        ).astype(BF16).reshape(1, CORES, TILES, SLOTS)
        for value in (place, number)
    ]


def local_grads(
    ids_hbm, pooled_hbm, pre_hbm, grad_hbm, w_hbm, out_ref, ids_ref, pooled_ref, pre_ref, grad_ref, w_ref, sems
):
    pairs = (
        (ids_hbm, ids_ref),
        (pre_hbm, pre_ref),
        (grad_hbm, grad_ref),
        (w_hbm, w_ref),
        (pooled_hbm, pooled_ref),
    )
    copies = [
        pltpu.make_async_copy(source, target, sems.at[i])
        for i, (source, target) in enumerate(pairs)
    ]
    for copy in copies:
        copy.start()
    copies[0].wait()
    place, number = slot_tables(ids_ref, pooled_ref.shape[0])
    shape = (PLANE // CORES, CORES, TILES, SLOTS)
    out_ref[:, 32:48, :] = jnp.broadcast_to(place, shape).reshape(PLANE, TILES, SLOTS)
    out_ref[:, 48:64, :] = jnp.broadcast_to(number, shape).reshape(PLANE, TILES, SLOTS)
    copies[1].wait()
    tanh_pre = jnp.tanh(pre_ref[...].astype(F32))
    copies[2].wait()
    derivative = (grad_ref[...].astype(F32) * (1.0 - tanh_pre * tanh_pre)).astype(BF16)
    copies[3].wait()
    pooled_t = lax.dot_general(
        w_ref[...], derivative, (((1,), (1,)), ((), ())), preferred_element_type=F32
    )
    out_ref[:, 64:80, :] = jnp.concatenate(
        [by_member(pooled_t[:, :LOW]), by_member(pooled_t[:, LOW:])], axis=1
    ).astype(BF16)
    copies[4].wait()
    dense = lax.dot_general(
        pooled_ref[...], derivative, (((0,), (0,)), ((), ())), preferred_element_type=F32
    )
    out_ref[:, 0:32, :] = jnp.concatenate(
        [by_member(dense[:, LOW * i : LOW * (i + 1)]) for i in range(4)], axis=1
    ).astype(BF16)


def decode(got_ref, source):
    place = got_ref[source, 32:48, :].astype(F32)
    number = got_ref[source, 48:64, :].astype(F32)
    grad = got_ref[source, 64:80, :].astype(F32)
    lane = jnp.maximum((jnp.abs(number) - 1.0) * 128.0, 0.0).astype(jnp.int32)
    high = jnp.zeros_like(place)
    scale = jnp.ones_like(place)
    for k in range(1, HIGH):
        above = place >= float(1 << k)
        high = jnp.where(above, float(k), high)
        scale = jnp.where(above, 1.0 / (1 << k), scale)
    low = (place * scale - 1.0) * 128.0
    return grad, lane, number < 0.0, place > 0.0, high, low


def merge_rows(got_ref, out_ref, total_ref):
    size = HIGH * COLS
    total_ref[...] = jnp.zeros_like(total_ref)
    second = (lax.broadcasted_iota(jnp.int32, (16, PAIR * SLOTS), 0) >= COLS).astype(F32)
    low_iota = lax.broadcasted_iota(jnp.int32, (LOW, PAIR * SLOTS), 0).astype(F32).astype(BF16)

    def product(tile, members):
        t = slice(tile, tile + 1)
        values, highs, lows = [], [], []
        for grad, lane, upper, filled, high, low in members:
            at = jnp.broadcast_to(lane[t], (COLS, SLOTS))
            value = jnp.where(
                upper[t],
                jnp.take_along_axis(grad[COLS:], at, axis=1),
                jnp.take_along_axis(grad[:COLS], at, axis=1),
            )
            values.append(jnp.where(filled[t], value, 0.0))
            highs.append(high[t])
            lows.append(low[t])
        value = jnp.concatenate(values, axis=1)
        value = jnp.concatenate([value, value], axis=0).astype(BF16)
        which = jnp.broadcast_to(jnp.concatenate(highs, axis=1), value.shape) - second
        which = which.astype(BF16)
        at_high = jnp.concatenate(
            [
                jnp.where(which == jnp.asarray(2 * k, BF16), value, jnp.zeros_like(value))
                for k in range(HIGH // 2)
            ],
            axis=0,
        )
        digit = jnp.broadcast_to(jnp.concatenate(lows, axis=1), low_iota.shape).astype(BF16)
        at_low = jnp.where(digit == low_iota, jnp.ones_like(digit), jnp.zeros_like(digit))
        return lax.dot_general(
            at_high, at_low, (((1,), (1,)), ((), ())), preferred_element_type=F32
        )

    def step(index, dense):
        pairs = []
        for pair in range(BATCH // PAIR):
            sources = [index * BATCH + pair * PAIR + member for member in range(PAIR)]
            pairs.append([decode(got_ref, source) for source in sources])
            for source in sources:
                dense += got_ref[source, 0:32, :].astype(F32)
        for tile in range(TILES):
            rows = slice(size * tile, size * (tile + 1))
            total = product(tile, pairs[0])
            for members in pairs[1:]:
                total += product(tile, members)
            total_ref[rows, :] += total
        return dense

    dense = lax.fori_loop(0, PLANE // BATCH, step, jnp.zeros((DENSE, LOW), F32))
    big = dense.astype(BF16)
    small = (dense - big.astype(F32)).astype(BF16)
    count = FAR * OWNED
    rows = total_ref[...].astype(BF16).reshape(FAR, NEAR, OWNED, LOW)
    for near in range(NEAR):
        out_ref[near, :count, :] = rows[:, near].reshape(count, LOW)
        out_ref[near, count : count + DENSE, :] = big
        out_ref[near, count + DENSE :, :] = small


def merge_near(got_ref, out_ref):
    total = jnp.sum(got_ref[...].astype(F32), axis=0)
    count = FAR * OWNED
    dense = total[count : count + DENSE] + total[count + DENSE :]
    out_ref[:, :OWNED, :] = total[:count].reshape(FAR, OWNED, LOW).astype(BF16)
    out_ref[:, OWNED:, :] = jnp.broadcast_to(dense.astype(BF16)[None], (FAR, DENSE, LOW))


def merge_far(got_ref, out_ref):
    total = jnp.sum(got_ref[...].astype(F32), axis=0).astype(BF16)
    out_ref[...] = jnp.broadcast_to(total[None], out_ref.shape)


def update_rows(got_ref, table_ref, accum_ref, table_out, accum_out, top_out):
    width = table_ref.shape[1]
    for h in range(OWNED // COLS):
        rows = from_members(got_ref, COLS * h)
        squares = jnp.sum(rows * rows, axis=0, keepdims=True) * (1.0 / width)
        new_accum = accum_ref[h : h + 1, :] + squares
        accum_out[h : h + 1, :] = new_accum
        change = (rows * (LEARN_RATE / (jnp.sqrt(new_accum) + ADA_EPS))).T
        at = slice(h * LOW, (h + 1) * LOW)
        table_out[at, :] = table_ref[at, :] - change
    for i in range(4):
        top_out[:, LOW * i : LOW * (i + 1)] = from_members(got_ref, OWNED + COLS * i)


def plane_of(place, near, core):
    far = FAR_ORDER[place]
    turned = (near + 2 * (far >= FAR // 2)) % NEAR
    return (far * NEAR + turned + 2 * core) % (FAR * NEAR)


def exchange(parts, axis, groups=None):
    return lax.all_to_all(
        parts, axis, split_axis=0, concat_axis=0, tiled=True, axis_index_groups=groups
    )


def local(ids, pooled, pre_act, grad_out, w_top, table, accum):
    both = ("shard", "replica")

    def place_of(far, near, member):
        return plane_of(far, near, member % CORES) * PLANE + member

    near_groups = [
        [place_of(f, n, member) for n in range(NEAR)] for member in range(PLANE) for f in range(FAR)
    ]
    far_groups = [
        [place_of(f, n, member) for f in range(FAR)] for member in range(PLANE) for n in range(NEAR)
    ]
    inputs = (ids.T, pooled, pre_act, grad_out, w_top)
    sent = call(
        local_grads,
        jax.ShapeDtypeStruct((PLANE, 80, LOW), BF16),
        inputs,
        scratch=[pltpu.VMEM(a.shape, a.dtype) for a in inputs]
        + [pltpu.SemaphoreType.DMA((5,))],
        memory=pl.ANY,
        vmem=64 * 1024 * 1024 - 256 * 1024,
    )
    got = exchange(sent, "replica", [list(PLANE_ORDER)])
    merged = call(
        merge_rows,
        jax.ShapeDtypeStruct((NEAR, FAR * OWNED + 2 * DENSE, LOW), BF16),
        (got,),
        scratch=(
            pltpu.VMEM((TILES * HIGH * COLS, LOW), F32),
        ),
    )
    got = exchange(merged, both, near_groups)
    merged = call(merge_near, jax.ShapeDtypeStruct((FAR, OWNED + DENSE, LOW), BF16), (got,))
    got = exchange(merged, both, far_groups)
    merged = call(merge_far, jax.ShapeDtypeStruct((PLANE, OWNED + DENSE, LOW), BF16), (got,))
    got = exchange(merged, "replica", [list(PLANE_ORDER)])
    rows = table.shape[0]
    new_table, new_accum, grad_top = call(
        update_rows,
        (
            jax.ShapeDtypeStruct(table.shape, F32),
            jax.ShapeDtypeStruct((rows // 128, 128), F32),
            jax.ShapeDtypeStruct(w_top.shape, F32),
        ),
        (got, table, accum.reshape(rows // 128, 128)),
    )
    return (new_table, new_accum.reshape(rows), grad_top)


def solution(mesh):
    return jax.shard_map(
        local,
        mesh=mesh,
        in_specs=(
            P(("shard", "replica"), None),
            P(("shard", "replica"), None),
            P(("shard", "replica"), None),
            P(("shard", "replica"), None),
            P(),
            P("shard", None),
            P("shard"),
        ),
        out_specs=(P("shard", None), P("shard"), P()),
        check_vma=False,
    )
```

```python
import jax
import jax.numpy as jnp
from jax import lax
from jax.experimental import pallas as pl
from jax.experimental.pallas import tpu as pltpu
from jax.sharding import PartitionSpec as P

LEARN_RATE = 0.5
ADA_EPS = 1e-08

BF16 = jnp.bfloat16
F32 = jnp.float32

PLANE = 32
COLS = 8
CORES = 2
NEAR = 4
FAR = 8
LOW = 128
HIGH = 16
TILES = 16
OWNERS = 2
CAP = 64
SLOTS = OWNERS * CAP
OWNED = 64
DENSE = 32
BATCH = 8
PAIR = 2
FAR_ORDER = (0, 4, 7, 3, 6, 2, 5, 1)
PLANE_ORDER = tuple(5 * k % PLANE for k in range(PLANE))
VMEM_BYTES = 40 * 1024 * 1024


def call(body, out_shape, args, scratch=(), memory=pltpu.VMEM, cost=None, vmem=VMEM_BYTES):
    return pl.pallas_call(
        body,
        out_shape=out_shape,
        in_specs=[pl.BlockSpec(memory_space=memory)] * len(args),
        out_specs=jax.tree.map(lambda _: pl.BlockSpec(memory_space=pltpu.VMEM), out_shape),
        scratch_shapes=list(scratch),
        cost_estimate=cost,
        compiler_params=pltpu.CompilerParams(vmem_limit_bytes=vmem),
    )(*args)


def code(number):
    size = (number & 127).astype(F32) * (1.0 / 128.0) + 1.0
    return jnp.where(number >= 128, -size, size)


def by_member(columns):
    blocks = [columns[COLS * p : COLS * (p + 1)] for p in PLANE_ORDER]
    return jnp.concatenate(blocks, axis=0).reshape(PLANE, COLS, LOW)


def from_members(got_ref, first):
    blocks = [
        got_ref[PLANE_ORDER.index(p), first : first + COLS, :].astype(F32) for p in range(PLANE)
    ]
    return jnp.concatenate(blocks, axis=0)


def slot_tables(ids_ref, samples):
    lookups = ids_ref.shape[0]
    total = lookups * samples
    ids = jnp.concatenate([ids_ref[j : j + 1, :] for j in range(lookups)], axis=1)
    owner = ids // (LOW * HIGH // OWNERS)
    named = (lax.broadcasted_iota(jnp.int32, (PLANE, total), 0) == owner).astype(F32)
    before = (
        lax.broadcasted_iota(jnp.int32, (samples, samples), 0)
        < lax.broadcasted_iota(jnp.int32, (samples, samples), 1)
    ).astype(F32)
    before = before.astype(BF16)
    ranks = []
    carry = jnp.zeros((PLANE, 1), F32)
    for j in range(lookups):
        part = named[:, j * samples : (j + 1) * samples]
        earlier = carry + jnp.dot(part.astype(BF16), before, preferred_element_type=F32)
        ranks.append(jnp.sum(part * earlier, axis=0, keepdims=True))
        carry += jnp.sum(part, axis=1, keepdims=True)
    slot = ((owner % OWNERS) * CAP).astype(F32) + jnp.concatenate(ranks, axis=1)
    place = code(ids % LOW) * (1 << ((ids // LOW) % HIGH)).astype(F32)
    number = code(lax.broadcasted_iota(jnp.int32, (1, total), 1) % samples)
    tile = owner // OWNERS
    kinds = [(tile + TILES - core) % TILES for core in range(CORES)]
    kinds = [kind ^ (kind // (TILES // 2)) for kind in kinds]
    kinds = [
        sum(jnp.where(kind // 2 == group, 2 * k, 0) for k, group in enumerate(FAR_ORDER))
        + kind % 2
        for kind in kinds
    ]
    tile = jnp.concatenate(
        [lax.broadcasted_iota(jnp.int32, (TILES, total), 0) == kind for kind in kinds], axis=0
    )
    tile = tile.astype(F32).astype(BF16)
    at_slot = lax.broadcasted_iota(jnp.int32, (SLOTS, total), 0).astype(F32) == slot
    return [
        lax.dot_general(
            tile,
            jnp.where(at_slot, value, 0.0).astype(BF16),
            (((1,), (1,)), ((), ())),
            preferred_element_type=F32,
        ).astype(BF16).reshape(1, CORES, TILES, SLOTS)
        for value in (place, number)
    ]


def local_grads(
    ids_hbm, pooled_hbm, pre_hbm, grad_hbm, w_hbm, out_ref, ids_ref, pooled_ref, pre_ref, grad_ref, w_ref, sems
):
    pairs = (
        (ids_hbm, ids_ref),
        (pre_hbm, pre_ref),
        (grad_hbm, grad_ref),
        (w_hbm, w_ref),
        (pooled_hbm, pooled_ref),
    )
    copies = [
        pltpu.make_async_copy(source, target, sems.at[i])
        for i, (source, target) in enumerate(pairs)
    ]
    for copy in copies:
        copy.start()
    copies[0].wait()
    place, number = slot_tables(ids_ref, pooled_ref.shape[0])
    shape = (PLANE // CORES, CORES, TILES, SLOTS)
    out_ref[:, 32:48, :] = jnp.broadcast_to(place, shape).reshape(PLANE, TILES, SLOTS)
    out_ref[:, 48:64, :] = jnp.broadcast_to(number, shape).reshape(PLANE, TILES, SLOTS)
    copies[1].wait()
    tanh_pre = jnp.tanh(pre_ref[...].astype(F32))
    copies[2].wait()
    derivative = (grad_ref[...].astype(F32) * (1.0 - tanh_pre * tanh_pre)).astype(BF16)
    copies[3].wait()
    pooled_t = lax.dot_general(
        w_ref[...], derivative, (((1,), (1,)), ((), ())), preferred_element_type=F32
    )
    out_ref[:, 64:80, :] = jnp.concatenate(
        [by_member(pooled_t[:, :LOW]), by_member(pooled_t[:, LOW:])], axis=1
    ).astype(BF16)
    copies[4].wait()
    dense = lax.dot_general(
        pooled_ref[...], derivative, (((0,), (0,)), ((), ())), preferred_element_type=F32
    )
    out_ref[:, 0:32, :] = jnp.concatenate(
        [by_member(dense[:, LOW * i : LOW * (i + 1)]) for i in range(4)], axis=1
    ).astype(BF16)


def decode(got_ref, source):
    place = got_ref[source, 32:48, :].astype(F32)
    number = got_ref[source, 48:64, :].astype(F32)
    grad = got_ref[source, 64:80, :].astype(F32)
    lane = jnp.maximum((jnp.abs(number) - 1.0) * 128.0, 0.0).astype(jnp.int32)
    high = jnp.zeros_like(place)
    scale = jnp.ones_like(place)
    for k in range(1, HIGH):
        above = place >= float(1 << k)
        high = jnp.where(above, float(k), high)
        scale = jnp.where(above, 1.0 / (1 << k), scale)
    low = (place * scale - 1.0) * 128.0
    return grad, lane, number < 0.0, place > 0.0, high, low


def merge_rows(got_ref, out_ref, total_ref):
    size = HIGH * COLS
    total_ref[...] = jnp.zeros_like(total_ref)
    second = (lax.broadcasted_iota(jnp.int32, (16, PAIR * SLOTS), 0) >= COLS).astype(F32)
    low_iota = lax.broadcasted_iota(jnp.int32, (LOW, PAIR * SLOTS), 0).astype(F32).astype(BF16)

    def product(tile, members):
        t = slice(tile, tile + 1)
        values, highs, lows = [], [], []
        for grad, lane, upper, filled, high, low in members:
            at = jnp.broadcast_to(lane[t], (COLS, SLOTS))
            value = jnp.where(
                upper[t],
                jnp.take_along_axis(grad[COLS:], at, axis=1),
                jnp.take_along_axis(grad[:COLS], at, axis=1),
            )
            values.append(jnp.where(filled[t], value, 0.0))
            highs.append(high[t])
            lows.append(low[t])
        value = jnp.concatenate(values, axis=1)
        value = jnp.concatenate([value, value], axis=0).astype(BF16)
        which = jnp.broadcast_to(jnp.concatenate(highs, axis=1), value.shape) - second
        which = which.astype(BF16)
        at_high = jnp.concatenate(
            [
                jnp.where(which == jnp.asarray(2 * k, BF16), value, jnp.zeros_like(value))
                for k in range(HIGH // 2)
            ],
            axis=0,
        )
        digit = jnp.broadcast_to(jnp.concatenate(lows, axis=1), low_iota.shape).astype(BF16)
        at_low = jnp.where(digit == low_iota, jnp.ones_like(digit), jnp.zeros_like(digit))
        return lax.dot_general(
            at_high, at_low, (((1,), (1,)), ((), ())), preferred_element_type=F32
        )

    def step(index, dense):
        pairs = []
        for pair in range(BATCH // PAIR):
            sources = [index * BATCH + pair * PAIR + member for member in range(PAIR)]
            pairs.append([decode(got_ref, source) for source in sources])
            for source in sources:
                dense += got_ref[source, 0:32, :].astype(F32)
        for tile in range(TILES):
            rows = slice(size * tile, size * (tile + 1))
            total = product(tile, pairs[0])
            for members in pairs[1:]:
                total += product(tile, members)
            total_ref[rows, :] += total
        return dense

    dense = lax.fori_loop(0, PLANE // BATCH, step, jnp.zeros((DENSE, LOW), F32))
    big = dense.astype(BF16)
    small = (dense - big.astype(F32)).astype(BF16)
    count = FAR * OWNED
    rows = total_ref[...].astype(BF16).reshape(FAR, NEAR, OWNED, LOW)
    for near in range(NEAR):
        out_ref[near, :count, :] = rows[:, near].reshape(count, LOW)
        out_ref[near, count : count + DENSE, :] = big
        out_ref[near, count + DENSE :, :] = small


def merge_near(got_ref, out_ref):
    total = jnp.sum(got_ref[...].astype(F32), axis=0)
    count = FAR * OWNED
    dense = total[count : count + DENSE] + total[count + DENSE :]
    out_ref[:, :OWNED, :] = total[:count].reshape(FAR, OWNED, LOW).astype(BF16)
    out_ref[:, OWNED:, :] = jnp.broadcast_to(dense.astype(BF16)[None], (FAR, DENSE, LOW))


def merge_far(got_ref, out_ref):
    total = jnp.sum(got_ref[...].astype(F32), axis=0)
    big = total.astype(BF16)
    small = (total[OWNED:] - big[OWNED:].astype(F32)).astype(BF16)
    out_ref[:, : OWNED + DENSE, :] = jnp.broadcast_to(big[None], (PLANE, OWNED + DENSE, LOW))
    out_ref[:, OWNED + DENSE :, :] = jnp.broadcast_to(small[None], (PLANE, DENSE, LOW))


def update_rows(got_ref, table_ref, accum_ref, table_out, accum_out, top_out):
    width = table_ref.shape[1]
    for h in range(OWNED // COLS):
        rows = from_members(got_ref, COLS * h)
        squares = jnp.sum(rows * rows, axis=0, keepdims=True) * (1.0 / width)
        new_accum = accum_ref[h : h + 1, :] + squares
        accum_out[h : h + 1, :] = new_accum
        change = (rows * (LEARN_RATE / (jnp.sqrt(new_accum) + ADA_EPS))).T
        at = slice(h * LOW, (h + 1) * LOW)
        table_out[at, :] = table_ref[at, :] - change
    for i in range(4):
        first = OWNED + COLS * i
        top_out[:, LOW * i : LOW * (i + 1)] = from_members(got_ref, first) + from_members(
            got_ref, first + DENSE
        )


def plane_of(place, near, core):
    far = FAR_ORDER[place]
    turned = (near + 2 * (far >= FAR // 2)) % NEAR
    return (far * NEAR + turned + 2 * core) % (FAR * NEAR)


def exchange(parts, axis, groups=None):
    return lax.all_to_all(
        parts, axis, split_axis=0, concat_axis=0, tiled=True, axis_index_groups=groups
    )


def local(ids, pooled, pre_act, grad_out, w_top, table, accum):
    both = ("shard", "replica")

    def place_of(far, near, member):
        return plane_of(far, near, member % CORES) * PLANE + member

    near_groups = [
        [place_of(f, n, member) for n in range(NEAR)] for member in range(PLANE) for f in range(FAR)
    ]
    far_groups = [
        [place_of(f, n, member) for f in range(FAR)] for member in range(PLANE) for n in range(NEAR)
    ]
    inputs = (ids.T, pooled, pre_act, grad_out, w_top)
    sent = call(
        local_grads,
        jax.ShapeDtypeStruct((PLANE, 80, LOW), BF16),
        inputs,
        scratch=[pltpu.VMEM(a.shape, a.dtype) for a in inputs]
        + [pltpu.SemaphoreType.DMA((5,))],
        memory=pl.ANY,
        vmem=64 * 1024 * 1024 - 256 * 1024,
    )
    got = exchange(sent, "replica", [list(PLANE_ORDER)])
    merged = call(
        merge_rows,
        jax.ShapeDtypeStruct((NEAR, FAR * OWNED + 2 * DENSE, LOW), BF16),
        (got,),
        scratch=(
            pltpu.VMEM((TILES * HIGH * COLS, LOW), F32),
        ),
    )
    got = exchange(merged, both, near_groups)
    merged = call(merge_near, jax.ShapeDtypeStruct((FAR, OWNED + DENSE, LOW), BF16), (got,))
    got = exchange(merged, both, far_groups)
    merged = call(merge_far, jax.ShapeDtypeStruct((PLANE, OWNED + 2 * DENSE, LOW), BF16), (got,))
    got = exchange(merged, "replica", [list(PLANE_ORDER)])
    rows = table.shape[0]
    new_table, new_accum, grad_top = call(
        update_rows,
        (
            jax.ShapeDtypeStruct(table.shape, F32),
            jax.ShapeDtypeStruct((rows // 128, 128), F32),
            jax.ShapeDtypeStruct(w_top.shape, F32),
        ),
        (got, table, accum.reshape(rows // 128, 128)),
    )
    return (new_table, new_accum.reshape(rows), grad_top)


def solution(mesh):
    return jax.shard_map(
        local,
        mesh=mesh,
        in_specs=(
            P(("shard", "replica"), None),
            P(("shard", "replica"), None),
            P(("shard", "replica"), None),
            P(("shard", "replica"), None),
            P(),
            P("shard", None),
            P("shard"),
        ),
        out_specs=(P("shard", None), P("shard"), P()),
        check_vma=False,
    )
```

```python
import jax
import jax.numpy as jnp
from jax import lax
from jax.experimental import pallas as pl
from jax.experimental.pallas import tpu as pltpu
from jax.sharding import PartitionSpec as P

LEARN_RATE = 0.5
ADA_EPS = 1e-08

BF16 = jnp.bfloat16
F32 = jnp.float32

PLANE = 32
COLS = 8
CORES = 2
NEAR = 4
FAR = 8
LOW = 128
HIGH = 16
TILES = 16
OWNERS = 2
CAP = 64
SLOTS = OWNERS * CAP
OWNED = 64
DENSE = 32
BATCH = 16
PAIR = 2
FAR_ORDER = (0, 4, 7, 3, 6, 2, 5, 1)
PLANE_ORDER = tuple(3 * k % PLANE for k in range(PLANE))
VMEM_BYTES = 40 * 1024 * 1024


def call(body, out_shape, args, scratch=(), memory=pltpu.VMEM, cost=None, vmem=VMEM_BYTES):
    return pl.pallas_call(
        body,
        out_shape=out_shape,
        in_specs=[pl.BlockSpec(memory_space=memory)] * len(args),
        out_specs=jax.tree.map(lambda _: pl.BlockSpec(memory_space=pltpu.VMEM), out_shape),
        scratch_shapes=list(scratch),
        cost_estimate=cost,
        compiler_params=pltpu.CompilerParams(vmem_limit_bytes=vmem),
    )(*args)


def code(number):
    size = (number & 127).astype(F32) * (1.0 / 128.0) + 1.0
    return jnp.where(number >= 128, -size, size)


def by_member(columns):
    blocks = [columns[COLS * p : COLS * (p + 1)] for p in PLANE_ORDER]
    return jnp.concatenate(blocks, axis=0).reshape(PLANE, COLS, LOW)


def from_members(got_ref, first):
    blocks = [
        got_ref[PLANE_ORDER.index(p), first : first + COLS, :].astype(F32) for p in range(PLANE)
    ]
    return jnp.concatenate(blocks, axis=0)


def slot_tables(ids_ref, samples):
    lookups = ids_ref.shape[0]
    total = lookups * samples
    ids = jnp.concatenate([ids_ref[j : j + 1, :] for j in range(lookups)], axis=1)
    owner = ids // (LOW * HIGH // OWNERS)
    named = (lax.broadcasted_iota(jnp.int32, (PLANE, total), 0) == owner).astype(F32)
    before = (
        lax.broadcasted_iota(jnp.int32, (samples, samples), 0)
        < lax.broadcasted_iota(jnp.int32, (samples, samples), 1)
    ).astype(F32)
    before = before.astype(BF16)
    ranks = []
    carry = jnp.zeros((PLANE, 1), F32)
    for j in range(lookups):
        part = named[:, j * samples : (j + 1) * samples]
        earlier = carry + jnp.dot(part.astype(BF16), before, preferred_element_type=F32)
        ranks.append(jnp.sum(part * earlier, axis=0, keepdims=True))
        carry += jnp.sum(part, axis=1, keepdims=True)
    slot = ((owner % OWNERS) * CAP).astype(F32) + jnp.concatenate(ranks, axis=1)
    place = code(ids % LOW) * (1 << ((ids // LOW) % HIGH)).astype(F32)
    number = code(lax.broadcasted_iota(jnp.int32, (1, total), 1) % samples)
    tile = owner // OWNERS
    kinds = [(tile + TILES - core) % TILES for core in range(CORES)]
    kinds = [kind ^ (kind // (TILES // 2)) for kind in kinds]
    kinds = [
        sum(jnp.where(kind // 2 == group, 2 * k, 0) for k, group in enumerate(FAR_ORDER))
        + kind % 2
        for kind in kinds
    ]
    tile = jnp.concatenate(
        [lax.broadcasted_iota(jnp.int32, (TILES, total), 0) == kind for kind in kinds], axis=0
    )
    tile = tile.astype(F32).astype(BF16)
    at_slot = lax.broadcasted_iota(jnp.int32, (SLOTS, total), 0).astype(F32) == slot
    return [
        lax.dot_general(
            tile,
            jnp.where(at_slot, value, 0.0).astype(BF16),
            (((1,), (1,)), ((), ())),
            preferred_element_type=F32,
        ).astype(BF16).reshape(1, CORES, TILES, SLOTS)
        for value in (place, number)
    ]


def local_grads(
    ids_hbm, pooled_hbm, pre_hbm, grad_hbm, w_hbm, out_ref, ids_ref, pooled_ref, pre_ref, grad_ref, w_ref, sems
):
    pairs = (
        (ids_hbm, ids_ref),
        (pre_hbm, pre_ref),
        (grad_hbm, grad_ref),
        (w_hbm, w_ref),
        (pooled_hbm, pooled_ref),
    )
    copies = [
        pltpu.make_async_copy(source, target, sems.at[i])
        for i, (source, target) in enumerate(pairs)
    ]
    for copy in copies:
        copy.start()
    copies[0].wait()
    place, number = slot_tables(ids_ref, pooled_ref.shape[0])
    shape = (PLANE // CORES, CORES, TILES, SLOTS)
    out_ref[:, 32:48, :] = jnp.broadcast_to(place, shape).reshape(PLANE, TILES, SLOTS)
    out_ref[:, 48:64, :] = jnp.broadcast_to(number, shape).reshape(PLANE, TILES, SLOTS)
    copies[1].wait()
    tanh_pre = jnp.tanh(pre_ref[...].astype(F32))
    copies[2].wait()
    derivative = (grad_ref[...].astype(F32) * (1.0 - tanh_pre * tanh_pre)).astype(BF16)
    copies[3].wait()
    pooled_t = lax.dot_general(
        w_ref[...], derivative, (((1,), (1,)), ((), ())), preferred_element_type=F32
    )
    out_ref[:, 64:80, :] = jnp.concatenate(
        [by_member(pooled_t[:, :LOW]), by_member(pooled_t[:, LOW:])], axis=1
    ).astype(BF16)
    copies[4].wait()
    dense = lax.dot_general(
        pooled_ref[...], derivative, (((0,), (0,)), ((), ())), preferred_element_type=F32
    )
    out_ref[:, 0:32, :] = jnp.concatenate(
        [by_member(dense[:, LOW * i : LOW * (i + 1)]) for i in range(4)], axis=1
    ).astype(BF16)


def decode(got_ref, source):
    place = got_ref[source, 32:48, :].astype(F32)
    number = got_ref[source, 48:64, :].astype(F32)
    grad = got_ref[source, 64:80, :].astype(F32)
    lane = jnp.maximum((jnp.abs(number) - 1.0) * 128.0, 0.0).astype(jnp.int32)
    high = jnp.zeros_like(place)
    scale = jnp.ones_like(place)
    for k in range(1, HIGH):
        above = place >= float(1 << k)
        high = jnp.where(above, float(k), high)
        scale = jnp.where(above, 1.0 / (1 << k), scale)
    low = (place * scale - 1.0) * 128.0
    return grad, lane, number < 0.0, place > 0.0, high, low


def merge_rows(got_ref, out_ref, total_ref):
    size = HIGH * COLS
    total_ref[...] = jnp.zeros_like(total_ref)
    second = (lax.broadcasted_iota(jnp.int32, (16, PAIR * SLOTS), 0) >= COLS).astype(F32)
    low_iota = lax.broadcasted_iota(jnp.int32, (LOW, PAIR * SLOTS), 0).astype(F32).astype(BF16)

    def product(tile, members):
        t = slice(tile, tile + 1)
        values, highs, lows = [], [], []
        for grad, lane, upper, filled, high, low in members:
            at = jnp.broadcast_to(lane[t], (COLS, SLOTS))
            value = jnp.where(
                upper[t],
                jnp.take_along_axis(grad[COLS:], at, axis=1),
                jnp.take_along_axis(grad[:COLS], at, axis=1),
            )
            values.append(jnp.where(filled[t], value, 0.0))
            highs.append(high[t])
            lows.append(low[t])
        value = jnp.concatenate(values, axis=1)
        value = jnp.concatenate([value, value], axis=0).astype(BF16)
        which = jnp.broadcast_to(jnp.concatenate(highs, axis=1), value.shape) - second
        which = which.astype(BF16)
        at_high = jnp.concatenate(
            [
                jnp.where(which == jnp.asarray(2 * k, BF16), value, jnp.zeros_like(value))
                for k in range(HIGH // 2)
            ],
            axis=0,
        )
        digit = jnp.broadcast_to(jnp.concatenate(lows, axis=1), low_iota.shape).astype(BF16)
        at_low = jnp.where(digit == low_iota, jnp.ones_like(digit), jnp.zeros_like(digit))
        return lax.dot_general(
            at_high, at_low, (((1,), (1,)), ((), ())), preferred_element_type=F32
        )

    def step(index, dense):
        pairs = []
        for pair in range(BATCH // PAIR):
            sources = [index * BATCH + pair * PAIR + member for member in range(PAIR)]
            pairs.append([decode(got_ref, source) for source in sources])
            for source in sources:
                dense += got_ref[source, 0:32, :].astype(F32)
        for tile in range(TILES):
            rows = slice(size * tile, size * (tile + 1))
            total = product(tile, pairs[0])
            for members in pairs[1:]:
                total += product(tile, members)
            total_ref[rows, :] += total
        return dense

    dense = lax.fori_loop(0, PLANE // BATCH, step, jnp.zeros((DENSE, LOW), F32))
    big = dense.astype(BF16)
    small = (dense - big.astype(F32)).astype(BF16)
    count = FAR * OWNED
    rows = total_ref[...].astype(BF16).reshape(FAR, NEAR, OWNED, LOW)
    for near in range(NEAR):
        out_ref[near, :count, :] = rows[:, near].reshape(count, LOW)
        out_ref[near, count : count + DENSE, :] = big
        out_ref[near, count + DENSE :, :] = small


def merge_near(got_ref, out_ref):
    total = jnp.sum(got_ref[...].astype(F32), axis=0)
    count = FAR * OWNED
    dense = total[count : count + DENSE] + total[count + DENSE :]
    out_ref[:, :OWNED, :] = total[:count].reshape(FAR, OWNED, LOW).astype(BF16)
    out_ref[:, OWNED:, :] = jnp.broadcast_to(dense.astype(BF16)[None], (FAR, DENSE, LOW))


def merge_far(got_ref, out_ref):
    total = jnp.sum(got_ref[...].astype(F32), axis=0).astype(BF16)
    out_ref[...] = jnp.broadcast_to(total[None], out_ref.shape)


def update_rows(got_ref, table_ref, accum_ref, table_out, accum_out, top_out):
    width = table_ref.shape[1]
    for h in range(OWNED // COLS):
        rows = from_members(got_ref, COLS * h)
        squares = jnp.sum(rows * rows, axis=0, keepdims=True) * (1.0 / width)
        new_accum = accum_ref[h : h + 1, :] + squares
        accum_out[h : h + 1, :] = new_accum
        change = (rows * (LEARN_RATE / (jnp.sqrt(new_accum) + ADA_EPS))).T
        at = slice(h * LOW, (h + 1) * LOW)
        table_out[at, :] = table_ref[at, :] - change
    for i in range(4):
        top_out[:, LOW * i : LOW * (i + 1)] = from_members(got_ref, OWNED + COLS * i)


def plane_of(place, near, core):
    far = FAR_ORDER[place]
    turned = (near + 2 * (far >= FAR // 2)) % NEAR
    return (far * NEAR + turned + 2 * core) % (FAR * NEAR)


def exchange(parts, axis, groups=None):
    return lax.all_to_all(
        parts, axis, split_axis=0, concat_axis=0, tiled=True, axis_index_groups=groups
    )


def local(ids, pooled, pre_act, grad_out, w_top, table, accum):
    both = ("shard", "replica")

    def place_of(far, near, member):
        return plane_of(far, near, member % CORES) * PLANE + member

    near_groups = [
        [place_of(f, n, member) for n in range(NEAR)] for member in range(PLANE) for f in range(FAR)
    ]
    far_groups = [
        [place_of(f, n, member) for f in range(FAR)] for member in range(PLANE) for n in range(NEAR)
    ]
    inputs = (ids.T, pooled, pre_act, grad_out, w_top)
    sent = call(
        local_grads,
        jax.ShapeDtypeStruct((PLANE, 80, LOW), BF16),
        inputs,
        scratch=[pltpu.VMEM(a.shape, a.dtype) for a in inputs]
        + [pltpu.SemaphoreType.DMA((5,))],
        memory=pl.ANY,
        vmem=64 * 1024 * 1024 - 256 * 1024,
    )
    got = exchange(sent, "replica", [list(PLANE_ORDER)])
    merged = call(
        merge_rows,
        jax.ShapeDtypeStruct((NEAR, FAR * OWNED + 2 * DENSE, LOW), BF16),
        (got,),
        scratch=(
            pltpu.VMEM((TILES * HIGH * COLS, LOW), F32),
        ),
    )
    got = exchange(merged, both, near_groups)
    merged = call(merge_near, jax.ShapeDtypeStruct((FAR, OWNED + DENSE, LOW), BF16), (got,))
    got = exchange(merged, both, far_groups)
    merged = call(merge_far, jax.ShapeDtypeStruct((PLANE, OWNED + DENSE, LOW), BF16), (got,))
    got = exchange(merged, "replica", [list(PLANE_ORDER)])
    rows = table.shape[0]
    new_table, new_accum, grad_top = call(
        update_rows,
        (
            jax.ShapeDtypeStruct(table.shape, F32),
            jax.ShapeDtypeStruct((rows // 128, 128), F32),
            jax.ShapeDtypeStruct(w_top.shape, F32),
        ),
        (got, table, accum.reshape(rows // 128, 128)),
    )
    return (new_table, new_accum.reshape(rows), grad_top)


def solution(mesh):
    return jax.shard_map(
        local,
        mesh=mesh,
        in_specs=(
            P(("shard", "replica"), None),
            P(("shard", "replica"), None),
            P(("shard", "replica"), None),
            P(("shard", "replica"), None),
            P(),
            P("shard", None),
            P("shard"),
        ),
        out_specs=(P("shard", None), P("shard"), P()),
        check_vma=False,
    )
```

```python
import jax
import jax.numpy as jnp
from jax import lax
from jax.experimental import pallas as pl
from jax.experimental.pallas import tpu as pltpu
from jax.sharding import PartitionSpec as P

LEARN_RATE = 0.5
ADA_EPS = 1e-08

BF16 = jnp.bfloat16
F32 = jnp.float32

PLANE = 32
COLS = 8
CORES = 2
NEAR = 4
FAR = 8
LOW = 128
HIGH = 16
TILES = 16
OWNERS = 2
CAP = 64
SLOTS = OWNERS * CAP
OWNED = 64
DENSE = 32
BATCH = 32
PAIR = 2
FAR_ORDER = (0, 4, 7, 3, 6, 2, 5, 1)
PLANE_ORDER = tuple(3 * k % PLANE for k in range(PLANE))
VMEM_BYTES = 40 * 1024 * 1024


def call(body, out_shape, args, scratch=(), memory=pltpu.VMEM, cost=None, vmem=VMEM_BYTES):
    return pl.pallas_call(
        body,
        out_shape=out_shape,
        in_specs=[pl.BlockSpec(memory_space=memory)] * len(args),
        out_specs=jax.tree.map(lambda _: pl.BlockSpec(memory_space=pltpu.VMEM), out_shape),
        scratch_shapes=list(scratch),
        cost_estimate=cost,
        compiler_params=pltpu.CompilerParams(vmem_limit_bytes=vmem),
    )(*args)


def code(number):
    size = (number & 127).astype(F32) * (1.0 / 128.0) + 1.0
    return jnp.where(number >= 128, -size, size)


def by_member(columns):
    blocks = [columns[COLS * p : COLS * (p + 1)] for p in PLANE_ORDER]
    return jnp.concatenate(blocks, axis=0).reshape(PLANE, COLS, LOW)


def from_members(got_ref, first):
    blocks = [
        got_ref[PLANE_ORDER.index(p), first : first + COLS, :].astype(F32) for p in range(PLANE)
    ]
    return jnp.concatenate(blocks, axis=0)


def slot_tables(ids_ref, samples):
    lookups = ids_ref.shape[0]
    total = lookups * samples
    ids = jnp.concatenate([ids_ref[j : j + 1, :] for j in range(lookups)], axis=1)
    owner = ids // (LOW * HIGH // OWNERS)
    named = (lax.broadcasted_iota(jnp.int32, (PLANE, total), 0) == owner).astype(F32)
    before = (
        lax.broadcasted_iota(jnp.int32, (samples, samples), 0)
        < lax.broadcasted_iota(jnp.int32, (samples, samples), 1)
    ).astype(F32)
    before = before.astype(BF16)
    ranks = []
    carry = jnp.zeros((PLANE, 1), F32)
    for j in range(lookups):
        part = named[:, j * samples : (j + 1) * samples]
        earlier = carry + jnp.dot(part.astype(BF16), before, preferred_element_type=F32)
        ranks.append(jnp.sum(part * earlier, axis=0, keepdims=True))
        carry += jnp.sum(part, axis=1, keepdims=True)
    slot = ((owner % OWNERS) * CAP).astype(F32) + jnp.concatenate(ranks, axis=1)
    place = code(ids % LOW) * (1 << ((ids // LOW) % HIGH)).astype(F32)
    number = code(lax.broadcasted_iota(jnp.int32, (1, total), 1) % samples)
    tile = owner // OWNERS
    kinds = [(tile + TILES - core) % TILES for core in range(CORES)]
    kinds = [kind ^ (kind // (TILES // 2)) for kind in kinds]
    kinds = [
        sum(jnp.where(kind // 2 == group, 2 * k, 0) for k, group in enumerate(FAR_ORDER))
        + kind % 2
        for kind in kinds
    ]
    tile = jnp.concatenate(
        [lax.broadcasted_iota(jnp.int32, (TILES, total), 0) == kind for kind in kinds], axis=0
    )
    tile = tile.astype(F32).astype(BF16)
    at_slot = lax.broadcasted_iota(jnp.int32, (SLOTS, total), 0).astype(F32) == slot
    return [
        lax.dot_general(
            tile,
            jnp.where(at_slot, value, 0.0).astype(BF16),
            (((1,), (1,)), ((), ())),
            preferred_element_type=F32,
        ).astype(BF16).reshape(1, CORES, TILES, SLOTS)
        for value in (place, number)
    ]


def local_grads(
    ids_hbm, pooled_hbm, pre_hbm, grad_hbm, w_hbm, out_ref, ids_ref, pooled_ref, pre_ref, grad_ref, w_ref, sems
):
    pairs = (
        (ids_hbm, ids_ref),
        (pre_hbm, pre_ref),
        (grad_hbm, grad_ref),
        (w_hbm, w_ref),
        (pooled_hbm, pooled_ref),
    )
    copies = [
        pltpu.make_async_copy(source, target, sems.at[i])
        for i, (source, target) in enumerate(pairs)
    ]
    for copy in copies:
        copy.start()
    copies[0].wait()
    place, number = slot_tables(ids_ref, pooled_ref.shape[0])
    shape = (PLANE // CORES, CORES, TILES, SLOTS)
    out_ref[:, 32:48, :] = jnp.broadcast_to(place, shape).reshape(PLANE, TILES, SLOTS)
    out_ref[:, 48:64, :] = jnp.broadcast_to(number, shape).reshape(PLANE, TILES, SLOTS)
    copies[1].wait()
    tanh_pre = jnp.tanh(pre_ref[...].astype(F32))
    copies[2].wait()
    derivative = (grad_ref[...].astype(F32) * (1.0 - tanh_pre * tanh_pre)).astype(BF16)
    copies[3].wait()
    pooled_t = lax.dot_general(
        w_ref[...], derivative, (((1,), (1,)), ((), ())), preferred_element_type=F32
    )
    out_ref[:, 64:80, :] = jnp.concatenate(
        [by_member(pooled_t[:, :LOW]), by_member(pooled_t[:, LOW:])], axis=1
    ).astype(BF16)
    copies[4].wait()
    dense = lax.dot_general(
        pooled_ref[...], derivative, (((0,), (0,)), ((), ())), preferred_element_type=F32
    )
    out_ref[:, 0:32, :] = jnp.concatenate(
        [by_member(dense[:, LOW * i : LOW * (i + 1)]) for i in range(4)], axis=1
    ).astype(BF16)


def decode(got_ref, source):
    place = got_ref[source, 32:48, :].astype(F32)
    number = got_ref[source, 48:64, :].astype(F32)
    grad = got_ref[source, 64:80, :].astype(F32)
    lane = jnp.maximum((jnp.abs(number) - 1.0) * 128.0, 0.0).astype(jnp.int32)
    high = jnp.zeros_like(place)
    scale = jnp.ones_like(place)
    for k in range(1, HIGH):
        above = place >= float(1 << k)
        high = jnp.where(above, float(k), high)
        scale = jnp.where(above, 1.0 / (1 << k), scale)
    low = (place * scale - 1.0) * 128.0
    return grad, lane, number < 0.0, place > 0.0, high, low


def merge_rows(got_ref, out_ref, total_ref):
    size = HIGH * COLS
    second = (lax.broadcasted_iota(jnp.int32, (16, PAIR * SLOTS), 0) >= COLS).astype(F32)
    low_iota = lax.broadcasted_iota(jnp.int32, (LOW, PAIR * SLOTS), 0).astype(F32).astype(BF16)

    def product(tile, members):
        t = slice(tile, tile + 1)
        values, highs, lows = [], [], []
        for grad, lane, upper, filled, high, low in members:
            at = jnp.broadcast_to(lane[t], (COLS, SLOTS))
            value = jnp.where(
                upper[t],
                jnp.take_along_axis(grad[COLS:], at, axis=1),
                jnp.take_along_axis(grad[:COLS], at, axis=1),
            )
            values.append(jnp.where(filled[t], value, 0.0))
            highs.append(high[t])
            lows.append(low[t])
        value = jnp.concatenate(values, axis=1)
        value = jnp.concatenate([value, value], axis=0).astype(BF16)
        which = jnp.broadcast_to(jnp.concatenate(highs, axis=1), value.shape) - second
        which = which.astype(BF16)
        at_high = jnp.concatenate(
            [
                jnp.where(which == jnp.asarray(2 * k, BF16), value, jnp.zeros_like(value))
                for k in range(HIGH // 2)
            ],
            axis=0,
        )
        digit = jnp.broadcast_to(jnp.concatenate(lows, axis=1), low_iota.shape).astype(BF16)
        at_low = jnp.where(digit == low_iota, jnp.ones_like(digit), jnp.zeros_like(digit))
        return lax.dot_general(
            at_high, at_low, (((1,), (1,)), ((), ())), preferred_element_type=F32
        )

    def step(index, dense):
        pairs = []
        for pair in range(BATCH // PAIR):
            sources = [index * BATCH + pair * PAIR + member for member in range(PAIR)]
            pairs.append([decode(got_ref, source) for source in sources])
            for source in sources:
                dense += got_ref[source, 0:32, :].astype(F32)
        for tile in range(TILES):
            rows = slice(size * tile, size * (tile + 1))
            total = product(tile, pairs[0])
            for members in pairs[1:]:
                total += product(tile, members)
            total_ref[rows, :] = total
        return dense

    dense = step(0, jnp.zeros((DENSE, LOW), F32))
    big = dense.astype(BF16)
    small = (dense - big.astype(F32)).astype(BF16)
    count = FAR * OWNED
    rows = total_ref[...].astype(BF16).reshape(FAR, NEAR, OWNED, LOW)
    for near in range(NEAR):
        out_ref[near, :count, :] = rows[:, near].reshape(count, LOW)
        out_ref[near, count : count + DENSE, :] = big
        out_ref[near, count + DENSE :, :] = small


def merge_near(got_ref, out_ref):
    total = jnp.sum(got_ref[...].astype(F32), axis=0)
    count = FAR * OWNED
    dense = total[count : count + DENSE] + total[count + DENSE :]
    out_ref[:, :OWNED, :] = total[:count].reshape(FAR, OWNED, LOW).astype(BF16)
    out_ref[:, OWNED:, :] = jnp.broadcast_to(dense.astype(BF16)[None], (FAR, DENSE, LOW))


def merge_far(got_ref, out_ref):
    total = jnp.sum(got_ref[...].astype(F32), axis=0).astype(BF16)
    out_ref[...] = jnp.broadcast_to(total[None], out_ref.shape)


def update_rows(got_ref, table_ref, accum_ref, table_out, accum_out, top_out):
    width = table_ref.shape[1]
    for h in range(OWNED // COLS):
        rows = from_members(got_ref, COLS * h)
        squares = jnp.sum(rows * rows, axis=0, keepdims=True) * (1.0 / width)
        new_accum = accum_ref[h : h + 1, :] + squares
        accum_out[h : h + 1, :] = new_accum
        change = (rows * (LEARN_RATE / (jnp.sqrt(new_accum) + ADA_EPS))).T
        at = slice(h * LOW, (h + 1) * LOW)
        table_out[at, :] = table_ref[at, :] - change
    for i in range(4):
        top_out[:, LOW * i : LOW * (i + 1)] = from_members(got_ref, OWNED + COLS * i)


def plane_of(place, near, core):
    far = FAR_ORDER[place]
    turned = (near + 2 * (far >= FAR // 2)) % NEAR
    return (far * NEAR + turned + 2 * core) % (FAR * NEAR)


def exchange(parts, axis, groups=None):
    return lax.all_to_all(
        parts, axis, split_axis=0, concat_axis=0, tiled=True, axis_index_groups=groups
    )


def local(ids, pooled, pre_act, grad_out, w_top, table, accum):
    both = ("shard", "replica")

    def place_of(far, near, member):
        return plane_of(far, near, member % CORES) * PLANE + member

    near_groups = [
        [place_of(f, n, member) for n in range(NEAR)] for member in range(PLANE) for f in range(FAR)
    ]
    far_groups = [
        [place_of(f, n, member) for f in range(FAR)] for member in range(PLANE) for n in range(NEAR)
    ]
    inputs = (ids.T, pooled, pre_act, grad_out, w_top)
    sent = call(
        local_grads,
        jax.ShapeDtypeStruct((PLANE, 80, LOW), BF16),
        inputs,
        scratch=[pltpu.VMEM(a.shape, a.dtype) for a in inputs]
        + [pltpu.SemaphoreType.DMA((5,))],
        memory=pl.ANY,
        vmem=64 * 1024 * 1024 - 256 * 1024,
    )
    got = exchange(sent, "replica", [list(PLANE_ORDER)])
    merged = call(
        merge_rows,
        jax.ShapeDtypeStruct((NEAR, FAR * OWNED + 2 * DENSE, LOW), BF16),
        (got,),
        scratch=(
            pltpu.VMEM((TILES * HIGH * COLS, LOW), F32),
        ),
    )
    got = exchange(merged, both, near_groups)
    merged = call(merge_near, jax.ShapeDtypeStruct((FAR, OWNED + DENSE, LOW), BF16), (got,))
    got = exchange(merged, both, far_groups)
    merged = call(merge_far, jax.ShapeDtypeStruct((PLANE, OWNED + DENSE, LOW), BF16), (got,))
    got = exchange(merged, "replica", [list(PLANE_ORDER)])
    rows = table.shape[0]
    new_table, new_accum, grad_top = call(
        update_rows,
        (
            jax.ShapeDtypeStruct(table.shape, F32),
            jax.ShapeDtypeStruct((rows // 128, 128), F32),
            jax.ShapeDtypeStruct(w_top.shape, F32),
        ),
        (got, table, accum.reshape(rows // 128, 128)),
    )
    return (new_table, new_accum.reshape(rows), grad_top)


def solution(mesh):
    return jax.shard_map(
        local,
        mesh=mesh,
        in_specs=(
            P(("shard", "replica"), None),
            P(("shard", "replica"), None),
            P(("shard", "replica"), None),
            P(("shard", "replica"), None),
            P(),
            P("shard", None),
            P("shard"),
        ),
        out_specs=(P("shard", None), P("shard"), P()),
        check_vma=False,
    )
```
